32 devices in a mesh: dp: 8 (over z, y), row: 2 (over core), col: 2 (over x).
Axes of the slice: x: 2, y: 2, z: 4, core: 2. Of those that a mesh axis runs over, the one named last changes fastest.
Arguments:
- tokens: bfloat16 [8192, 1024], P('dp', ('row', 'col')), may hold values from -6 to 6
- cotangent: bfloat16 [8192, 1024], P('dp', ('row', 'col')), may hold values from -6 to 6
- lengths: int32 [8, 4], P('dp'), may hold values from 1 to 800, 1024 in all within a row
- norm_gain: float32 [1024], replicated, may hold values from 0.5 to 1.5
- w_query: bfloat16 [1024, 1024], P(None, ('row', 'col')), may hold values from -0.1875 to 0.1875
- w_key: bfloat16 [1024, 1024], P(None, ('row', 'col')), may hold values from -0.1875 to 0.1875
- w_value: bfloat16 [1024, 2048], P(None, ('row', 'col')), may hold values from -0.1875 to 0.1875
- w_alpha: bfloat16 [1024, 8], P(None, ('row', 'col')), may hold values from -0.1875 to 0.1875
- w_beta: bfloat16 [1024, 8], P(None, ('row', 'col')), may hold values from -0.1875 to 0.1875
- conv_query: float32 [4, 1024], P(None, ('row', 'col')), may hold values from 0.2 to 1
- conv_key: float32 [4, 1024], P(None, ('row', 'col')), may hold values from 0.2 to 1
- conv_value: float32 [4, 2048], P(None, ('row', 'col')), may hold values from 0.2 to 1
- decay_log: float32 [8], P(('row', 'col')), may hold values from -6 to -1
- decay_bias: float32 [8], P(('row', 'col')), may hold values from -1.5 to 1
- w_outgate: bfloat16 [1024, 2048], P(None, ('row', 'col')), may hold values from -0.1875 to 0.1875
- out_gain: float32 [256], replicated, may hold values from 0.5 to 1.5
- w_out: bfloat16 [2048, 1024], P(('row', 'col')), may hold values from -0.125 to 0.125
- ffn_gain: float32 [1024], replicated, may hold values from 0.5 to 1.5
- w_gate: bfloat16 [1024, 2816], P(None, ('row', 'col')), may hold values from -0.1875 to 0.1875
- w_up: bfloat16 [1024, 2816], P(None, ('row', 'col')), may hold values from -0.1875 to 0.1875
- w_down: bfloat16 [2816, 1024], P(('row', 'col')), may hold values from -0.109375 to 0.109375
Outputs:
- output: bfloat16 [8192, 1024], P('dp', ('row', 'col'))
- input_grad: bfloat16 [8192, 1024], P('dp', ('row', 'col'))
- norm_gain_grad: float32 [1024], replicated
- w_query_grad: float32 [1024, 1024], P(None, ('row', 'col'))
- w_key_grad: float32 [1024, 1024], P(None, ('row', 'col'))
- w_value_grad: float32 [1024, 2048], P(None, ('row', 'col'))
- w_alpha_grad: float32 [1024, 8], P(None, ('row', 'col'))
- w_beta_grad: float32 [1024, 8], P(None, ('row', 'col'))
- conv_query_grad: float32 [4, 1024], P(None, ('row', 'col'))
- conv_key_grad: float32 [4, 1024], P(None, ('row', 'col'))
- conv_value_grad: float32 [4, 2048], P(None, ('row', 'col'))
- decay_log_grad: float32 [8], P(('row', 'col'))
- decay_bias_grad: float32 [8], P(('row', 'col'))
- w_outgate_grad: float32 [1024, 2048], P(None, ('row', 'col'))
- out_gain_grad: float32 [256], replicated
- w_out_grad: float32 [2048, 1024], P(('row', 'col'))
- ffn_gain_grad: float32 [1024], replicated
- w_gate_grad: float32 [1024, 2816], P(None, ('row', 'col'))
- w_up_grad: float32 [1024, 2816], P(None, ('row', 'col'))
- w_down_grad: float32 [2816, 1024], P(('row', 'col'))
The draws below stay inside these ranges and needn't reach their ends.
Inputs may be any that keep to these rules, and one draw needn't show every extreme that they name: Each row holds the lengths of 4 documents that together fill one sequence of 1024 tokens; the longest of each row is exactly 800.
All inputs are finite; a program needn't handle non-finite values.
Results may differ from the reference program's by a relative error of at most 0.017.
Values may be sent and summed in bfloat16 or wider, within the bound.
No kernel may reach another device: no remote copies, remote signals or barrier semaphores. Data moves between devices by JAX's collectives and lax.ppermute only.
A program may use at most 192 MiB of HBM per device.

```python
import math
import jax
import jax.numpy as jnp
import numpy as np
from jax import lax

D = 1024
H = 8
KH = 128
VH = 256
FF = 2816
CONV = 4
SPAN = 64
SEQ_LEN = 1024
DOCS = 4
DOC_MOST = 800
KEYDIM = 1024
VALDIM = 2048
SEQS = 8
TOKENS = 8192


def shard_levels(key, extent, cuts, least, high):
    loudness = 1.0
    for dim, shards_of in cuts:
        steps = jax.random.uniform(jax.random.fold_in(jax.random.fold_in(key, 6), dim), (shards_of,), jnp.float32, least / len(cuts), high / len(cuts))
        loudness = loudness * jnp.repeat(jnp.exp(steps), extent[dim] // shards_of).reshape((-1,) + (1,) * (len(extent) - 1 - dim))
    return loudness


def profile(amount, total, bound, skew):
    weights = [(1 << 20) // math.isqrt(grade ** skew) + 1 for grade in range(2, amount + 1)]
    rest, given = total - bound - (amount - 1), [1] * (amount - 1)
    while rest > 0:
        free = [i for i in range(amount - 1) if given[i] < bound]
        pool, budget = sum([weights[i] for i in free]), rest
        for i in free:
            extra = min(bound - given[i], max(1, budget * weights[i] // pool), rest)
            given[i] = given[i] + extra
            rest = rest - extra
    return np.array([bound] + given)


def ragged_sizes(own_key, number_of, total, reach, slope):
    if number_of == 2:
        one = jax.random.randint(own_key, (), max(1, total - reach), min(reach, total - 1) + 1)
        return jnp.stack([one, total - one])
    sizes = jnp.asarray(profile(number_of, total, reach, slope), jnp.int32)
    twos = (number_of - 1) // 2
    giver, receiver = sizes[1:1 + 2 * twos:2], sizes[2:2 + 2 * twos:2]
    room = jnp.minimum(giver - 1, reach - receiver)
    moved = jax.random.randint(jax.random.fold_in(own_key, 1), (twos,), 0, 1 << 20) % (room + 1)
    sizes = sizes.at[1:1 + 2 * twos:2].set(giver - moved).at[2:2 + 2 * twos:2].set(receiver + moved)
    return sizes[jax.random.permutation(jax.random.fold_in(own_key, 2), number_of)]


def normal_values(key, extent, deviation, limit, cuts=(), kind=jnp.bfloat16):
    level = shard_levels(key, extent, cuts, -0.22, 0.18) if cuts else 1.0
    entries = jax.random.normal(key, extent, jnp.float32) * deviation * level
    return jnp.minimum(jnp.maximum(entries, -limit), limit).astype(kind)


def setup_inputs(seed: int = 0) -> dict:
    key_list = jax.random.split(jax.random.key(seed), 22)
    return {
        "tokens": normal_values(key_list[0], (TOKENS, D), 1.0, 6.0, ((0, 8), (1, 4))),
        "cotangent": normal_values(key_list[1], (TOKENS, D), 1.0, 6.0, ((0, 8), (1, 4))),
        "lengths": jax.vmap(lambda own: ragged_sizes(own, DOCS, SEQ_LEN, DOC_MOST, 2))(jax.random.split(key_list[2], SEQS)).reshape((SEQS, DOCS)).astype(jnp.int32),
        "norm_gain": jnp.clip(1.0 + 0.1 * jax.random.normal(key_list[3], (D,), jnp.float32), 0.5, 1.5),
        "w_query": normal_values(key_list[4], (D, KEYDIM), D ** -0.5, 0.1875, ((1, 4),)),
        "w_key": normal_values(key_list[5], (D, KEYDIM), D ** -0.5, 0.1875, ((1, 4),)),
        "w_value": normal_values(key_list[6], (D, VALDIM), D ** -0.5, 0.1875, ((1, 4),)),
        "w_alpha": normal_values(key_list[7], (D, H), D ** -0.5, 0.1875, ((1, 4),)),
        "w_beta": normal_values(key_list[8], (D, H), D ** -0.5, 0.1875, ((1, 4),)),
        "conv_query": jnp.clip(0.2 + 0.8 * jax.random.uniform(key_list[9], (CONV, KEYDIM), jnp.float32) ** shard_levels(key_list[9], (CONV, KEYDIM), ((1, 4),), -0.2, 0.2), 0.2, 1.0),
        "conv_key": jnp.clip(0.2 + 0.8 * jax.random.uniform(key_list[10], (CONV, KEYDIM), jnp.float32) ** shard_levels(key_list[10], (CONV, KEYDIM), ((1, 4),), -0.2, 0.2), 0.2, 1.0),
        "conv_value": jnp.clip(0.2 + 0.8 * jax.random.uniform(key_list[11], (CONV, VALDIM), jnp.float32) ** shard_levels(key_list[11], (CONV, VALDIM), ((1, 4),), -0.2, 0.2), 0.2, 1.0),
        "decay_log": jnp.clip(-6.0 + 5.0 * jax.random.uniform(key_list[12], (H,), jnp.float32) ** shard_levels(key_list[12], (H,), ((0, 4),), -0.2, 0.2), -6.0, -1.0),
        "decay_bias": jnp.clip(-1.5 + 2.5 * jax.random.uniform(key_list[13], (H,), jnp.float32) ** shard_levels(key_list[13], (H,), ((0, 4),), -0.2, 0.2), -1.5, 1.0),
        "w_outgate": normal_values(key_list[14], (D, VALDIM), D ** -0.5, 0.1875, ((1, 4),)),
        "out_gain": jnp.clip(1.0 + 0.1 * jax.random.normal(key_list[15], (VH,), jnp.float32), 0.5, 1.5),
        "w_out": normal_values(key_list[16], (VALDIM, D), VALDIM ** -0.5, 0.125, ((0, 4),)),
        "ffn_gain": jnp.clip(1.0 + 0.1 * jax.random.normal(key_list[17], (D,), jnp.float32), 0.5, 1.5),
        "w_gate": normal_values(key_list[18], (D, FF), D ** -0.5, 0.1875, ((1, 4),)),
        "w_up": normal_values(key_list[19], (D, FF), D ** -0.5, 0.1875, ((1, 4),)),
        "w_down": normal_values(key_list[20], (FF, D), FF ** -0.5, 0.109375, ((0, 4),)),
    }


epsilon = 1e-06
out_epsilon = 0.05
highest = lax.Precision.HIGHEST

@jax.custom_vjp
def low(v):
    return lax.optimization_barrier(v.astype(jnp.bfloat16)).astype(jnp.float32)

@jax.custom_vjp
def low_back(v):
    return v

def low_keep(v):
    return (low(v), None)

def low_pass(kept, grad):
    return (grad,)

def back_keep(v):
    return (v, None)

def back_low(kept, grad):
    return (low(grad),)
low.defvjp(low_keep, low_pass)
low_back.defvjp(back_keep, back_low)

def matmul(matrix, factor):
    return jnp.dot(matrix, factor, precision=highest)

def rms_scale(values, scales):
    return values * lax.rsqrt(lax.optimization_barrier(jnp.mean(values * values, axis=-1, keepdims=True)) + epsilon) * scales

def head_scale(values, scales):
    return values * lax.rsqrt(lax.optimization_barrier(jnp.mean(values * values, axis=-1, keepdims=True)) + out_epsilon) * scales

def segments_of(lengths):
    doc_ends = jnp.cumsum(lengths.astype(jnp.int32), axis=-1, dtype=jnp.int32).astype(jnp.int32)
    places = jnp.arange(SEQ_LEN, dtype=jnp.int32)
    counted = (places[None, :, None] >= doc_ends[:, None, :]).astype(jnp.int32)
    return lax.optimization_barrier(jnp.sum(counted, axis=-1, dtype=jnp.int32)).astype(jnp.int32)

def short_conv(values, kernel, segment):
    summed = values * kernel[CONV - 1]
    for offset in range(1, CONV):
        shifted = jnp.pad(values[:, :-offset], ((0, 0), (offset, 0), (0, 0)))
        before = jnp.pad(segment[:, :-offset], ((0, 0), (offset, 0)), constant_values=-1)
        linked = (before == segment).astype(jnp.float32)
        summed = summed + shifted * linked[..., None] * kernel[CONV - 1 - offset]
    return jax.nn.silu(summed)

def to_blocks(values, seq_count, block_count, head_count):
    return jnp.moveaxis(values.reshape(seq_count, block_count, SPAN, head_count, -1), 3, 1)

def delta_rule(queries, key_heads, values, beta_rate, decay_rate, segment):
    seq_count, length, head_count = (queries.shape[0], queries.shape[1], queries.shape[2])
    block_count = length // SPAN
    query_b = to_blocks(queries, seq_count, block_count, head_count)
    key_b = to_blocks(key_heads, seq_count, block_count, head_count)
    value_b = to_blocks(values, seq_count, block_count, head_count)
    beta_b = to_blocks(beta_rate[..., None], seq_count, block_count, head_count)[..., 0]
    cumulative = jnp.cumsum(to_blocks(decay_rate[..., None], seq_count, block_count, head_count)[..., 0], axis=-1)
    seg_b = segment.reshape(seq_count, block_count, SPAN).astype(jnp.int32)
    before = jnp.concatenate([jnp.full((seq_count, 1), -1, jnp.int32), seg_b[:, :-1, -1].astype(jnp.int32)], axis=1)
    carried = (seg_b == before[..., None]).astype(jnp.float32)[:, None]
    positions = jnp.arange(SPAN, dtype=jnp.int32)
    below_mask = positions[:, None] >= positions[None, :]
    strict = (positions[:, None] > positions[None, :]).astype(jnp.float32)
    linked = ((seg_b[..., :, None] == seg_b[..., None, :]) & below_mask)[:, None]
    spread = cumulative[..., :, None] - cumulative[..., None, :]
    within = jnp.where(linked, jnp.exp(jnp.where(linked, spread, 0.0)), 0.0)
    key_gram = jnp.einsum('shncd,shnmd->shncm', key_b, key_b, precision=highest)
    system = jnp.eye(SPAN, dtype=jnp.float32) + beta_b[..., None] * within * strict * key_gram
    initial = jnp.exp(cumulative) * carried
    pseudo = lax.linalg.triangular_solve(system, beta_b[..., None] * value_b, left_side=True, lower=True, unit_diagonal=True)
    correct = lax.linalg.triangular_solve(system, (beta_b * initial)[..., None] * key_b, left_side=True, lower=True, unit_diagonal=True)
    scores = jnp.einsum('shncd,shnmd->shncm', query_b, key_b, precision=highest) * within
    tail_mask = (seg_b == seg_b[..., -1:]).astype(jnp.float32)[:, None]
    tail_decay = jnp.exp(cumulative[..., -1:] - cumulative) * tail_mask
    end_decay = jnp.exp(cumulative[..., -1]) * carried[..., -1]

    def advance(memory, pieces):
        pseudo_c, correct_c, query_c, key_c, scores_c, initial_c, tail_c, end_c = pieces
        delta_value = pseudo_c - jnp.einsum('shck,shvk->shcv', correct_c, memory, precision=highest)
        result = jnp.einsum('shck,shvk->shcv', initial_c[..., None] * query_c, memory, precision=highest)
        result = result + jnp.einsum('shcm,shmv->shcv', scores_c, delta_value, precision=highest)
        memory = end_c[..., None, None] * memory + jnp.einsum('shcv,shck->shvk', tail_c[..., None] * delta_value, key_c, precision=highest)
        return (memory, result)

    def leading(array):
        return jnp.moveaxis(array, 2, 0)
    memory = jnp.zeros((seq_count, head_count, values.shape[-1], queries.shape[-1]), jnp.float32)
    pieces = tuple((leading(item) for item in (pseudo, correct, query_b, key_b, scores, initial, tail_decay, end_decay)))
    memory, results = lax.scan(advance, memory, pieces)
    results = jnp.moveaxis(jnp.moveaxis(results, 0, 2), 1, 3)
    return results.reshape(seq_count, length, head_count, -1)

def mixer_core(query_proj, key_proj, value_proj, alpha_proj, beta_proj, gate_proj, conv_query, conv_key, conv_value, decay_log, decay_bias, out_gain, segment):
    seq_count, length = segment.shape
    head_count = alpha_proj.shape[-1]
    queries = short_conv(query_proj, conv_query, segment).reshape(seq_count, length, head_count, KH)
    key_heads = short_conv(key_proj, conv_key, segment).reshape(seq_count, length, head_count, KH)
    key_heads = key_heads * lax.rsqrt(lax.optimization_barrier(jnp.sum(key_heads * key_heads, axis=-1, keepdims=True)) + epsilon)
    values = short_conv(value_proj, conv_value, segment).reshape(seq_count, length, head_count, VH)
    beta_rate = jax.nn.sigmoid(beta_proj)
    decay_rate = -jnp.exp(decay_log) * jax.nn.softplus(alpha_proj + decay_bias)
    result = delta_rule(queries, key_heads, values, beta_rate, decay_rate, segment)
    gate_act = jax.nn.silu(gate_proj.reshape(seq_count, length, head_count, VH))
    normed = head_scale(result, out_gain) * gate_act
    return normed.reshape(seq_count, length, head_count * VH)

def layer_block(inputs, lengths, weights):
    norm_gain, w_query, w_key, w_value, w_alpha, w_beta, conv_query, conv_key, conv_value, decay_log, decay_bias, w_outgate, out_gain, w_out, ffn_gain, w_gate, w_up, w_down = weights
    segment = segments_of(lengths)
    normed = low(rms_scale(inputs, norm_gain))
    query_proj = low_back(matmul(normed, w_query))
    key_proj = low_back(matmul(normed, w_key))
    value_proj = low_back(matmul(normed, w_value))
    alpha_proj = low_back(matmul(normed, w_alpha))
    beta_proj = low_back(matmul(normed, w_beta))
    gate_proj = low_back(matmul(normed, w_outgate))
    mixed = low(mixer_core(query_proj, key_proj, value_proj, alpha_proj, beta_proj, gate_proj, conv_query, conv_key, conv_value, decay_log, decay_bias, out_gain, segment))
    hidden = low_back(inputs + matmul(mixed, w_out))
    normed_ffn = low(rms_scale(hidden, ffn_gain))
    gate_act = low_back(matmul(normed_ffn, w_gate))
    up_act = low_back(matmul(normed_ffn, w_up))
    product = low(jax.nn.silu(gate_act) * up_act)
    return hidden + matmul(product, w_down)

def reference(tokens, cotangent, lengths, norm_gain, w_query, w_key, w_value, w_alpha, w_beta, conv_query, conv_key, conv_value, decay_log, decay_bias, w_outgate, out_gain, w_out, ffn_gain, w_gate, w_up, w_down):
    params = (norm_gain, w_query, w_key, w_value, w_alpha, w_beta, conv_query, conv_key, conv_value, decay_log, decay_bias, w_outgate, out_gain, w_out, ffn_gain, w_gate, w_up, w_down)
    floats = tuple((weight.astype(jnp.float32) for weight in params))
    total_seqs = lengths.shape[0]
    group_size = math.gcd(total_seqs, 4)
    lengths_int = lengths.astype(jnp.int32)

    def forward(inputs, *weights):
        grouped = inputs.reshape(total_seqs // group_size, group_size, SEQ_LEN, inputs.shape[-1])
        lengths_grouped = lengths_int.reshape(total_seqs // group_size, group_size, lengths.shape[-1])

        def one_group(pieces):
            return layer_block(pieces[0], pieces[1], weights)
        result = lax.map(jax.checkpoint(one_group), (grouped, lengths_grouped))
        return result.reshape(total_seqs * SEQ_LEN, inputs.shape[-1])
    output, pullback = jax.vjp(forward, tokens.astype(jnp.float32), *floats)
    gradients = pullback(cotangent.astype(jnp.float32))
    return (output.astype(jnp.bfloat16), gradients[0].astype(jnp.bfloat16), gradients[1], gradients[2], gradients[3], gradients[4], gradients[5], gradients[6], gradients[7], gradients[8], gradients[9], gradients[10], gradients[11], gradients[12], gradients[13], gradients[14], gradients[15], gradients[16], gradients[17], gradients[18])
```

```python
import functools

import jax
import jax.numpy as jnp
from jax import lax
from jax.experimental import pallas as pl
from jax.experimental.pallas import tpu as pltpu
from jax.sharding import PartitionSpec as P

KH = 128
VH = 256
CONV = 4
BLOCK = 128
TAIL = 128

epsilon = 1e-06
out_epsilon = 0.05

NN = (((1,), (0,)), ((), ()))
NT = (((1,), (1,)), ((), ()))
TN = (((0,), (0,)), ((), ()))


def product_one(first, second, dims=NN):
    return lax.dot_general(
        first.astype(jnp.bfloat16),
        second.astype(jnp.bfloat16),
        dims,
        preferred_element_type=jnp.float32,
    )


def product_three(first, second, dims=NN):
    first_high = first.astype(jnp.bfloat16)
    second_high = second.astype(jnp.bfloat16)
    first_low = (first - first_high.astype(jnp.float32)).astype(jnp.bfloat16)
    second_low = (second - second_high.astype(jnp.float32)).astype(jnp.bfloat16)
    dot = functools.partial(
        lax.dot_general, dimension_numbers=dims, preferred_element_type=jnp.float32
    )
    return dot(first_high, second_high) + (
        dot(first_high, second_low) + dot(first_low, second_high)
    )


def product_six(first, second, dims=NN):
    return lax.dot_general(
        first, second, dims, precision=lax.Precision.HIGHEST, preferred_element_type=jnp.float32
    )


mm_sum = product_six
mm_inverse = product_three
mm_chain = product_three
mm_gram = product_three
mm_out = product_three
mm_back = product_three


def sigmoid(values):
    return 1.0 / (1.0 + jnp.exp(-values))


def softplus(values):
    return jnp.maximum(values, 0.0) + jnp.log1p(jnp.exp(-jnp.abs(values)))


def document_starts(lengths_ref, positions):
    starts = jnp.zeros_like(positions)
    end = 0
    for doc in range(lengths_ref.shape[1] - 1):
        end = end + lengths_ref[0, doc]
        starts = jnp.where(positions >= end, end, starts)
    return starts


def start_of(lengths_ref, position):
    start = 0
    end = 0
    for doc in range(lengths_ref.shape[1] - 1):
        end = end + lengths_ref[0, doc]
        start = jnp.where(position >= end, end, start)
    return start


def unit_inverses(lowers):
    size = lowers[0].shape[0]
    row = lax.broadcasted_iota(jnp.int32, (size, size), 0)
    column = lax.broadcasted_iota(jnp.int32, (size, size), 1)
    eye = (row == column).astype(jnp.float32)
    within = (row >> 3) == (column >> 3)
    inner = [jnp.where(within, low, 0.0) for low in lowers]
    square = [mm_inverse(one, one) for one in inner]
    cube = [mm_inverse(one, two) for one, two in zip(inner, square)]
    fourth = [mm_inverse(two, two) for two in square]
    part = [eye - one + two - three for one, two, three in zip(inner, square, cube)]
    result = [one + mm_inverse(one, four) for one, four in zip(part, fourth)]
    shift = 3
    while (1 << shift) < size:
        off = ((row >> (shift + 1)) == (column >> (shift + 1))) & (
            (row >> shift) != (column >> shift)
        )
        edge = [mm_inverse(jnp.where(off, low, 0.0), one) for low, one in zip(lowers, result)]
        result = [one - mm_inverse(one, two) for one, two in zip(result, edge)]
        shift += 1
    return result


def window_before(ref, start, columns):
    early = pl.multiple_of(jnp.maximum(start - 8, 0), 8)
    return jnp.concatenate(
        [ref[pl.ds(early, 8), columns], ref[pl.ds(start, BLOCK), columns]], axis=0
    )


def decays(tail, scales, biases):
    logits = tail + biases
    return -jnp.exp(scales) * softplus(logits), logits


def block_masks(lengths_ref, start):
    positions = start + lax.broadcasted_iota(jnp.int32, (BLOCK, 1), 0)
    starts = document_starts(lengths_ref, positions)
    columns = start + lax.broadcasted_iota(jnp.int32, (BLOCK, BLOCK), 1)
    rows = start + lax.broadcasted_iota(jnp.int32, (BLOCK, BLOCK), 0)
    linked = (starts <= columns) & (rows >= columns)
    strict = rows > columns
    carried = (starts < start).astype(jnp.float32)
    last_start = start_of(lengths_ref, start + BLOCK - 1)
    tail_mask = (positions >= last_start).astype(jnp.float32)
    last_carried = (last_start < start).astype(jnp.float32)
    return positions - starts, linked, strict, carried, tail_mask, last_carried


def lower_ones():
    row = lax.broadcasted_iota(jnp.int32, (BLOCK, BLOCK), 0)
    column = lax.broadcasted_iota(jnp.int32, (BLOCK, BLOCK), 1)
    return (row >= column).astype(jnp.float32)


def head_decay(cumulative, flipped, head, linked, carried, tail_mask, last_carried):
    cum = cumulative[:, head : head + 1]
    spread = cum - flipped[head : head + 1, :]
    within = jnp.where(linked, jnp.exp(jnp.where(linked, spread, 0.0)), 0.0)
    last = cumulative[BLOCK - 1 : BLOCK, head : head + 1]
    initial = jnp.exp(cum) * carried
    tail = jnp.exp(last - cum) * tail_mask
    end = jnp.exp(last) * last_carried
    return within, initial, tail, end


def forward_kernel(
    heads,
    lengths_ref,
    proj_ref,
    filter_ref,
    decay_ref,
    gain_ref,
    mixed_ref,
    act_ref,
    inverse_ref,
    state_ref,
    delta_ref,
    result_ref,
    score_ref,
    gram_ref,
    query_ref,
    step_ref,
    pseudo_ref,
    correct_ref,
    add_ref,
):
    length = proj_ref.shape[0]
    blocks = length // BLOCK
    key_dim, value_dim = heads * KH, heads * VH
    tail_at = 2 * key_dim + 2 * value_dim
    widths = ((0, key_dim), (key_dim, 2 * key_dim), (2 * key_dim, 2 * key_dim + value_dim))

    def first(block, _):
        start = pl.multiple_of(block * BLOCK, BLOCK)
        rows = pl.ds(start, BLOCK)
        since, linked, strict, carried, tail_mask, last_carried = block_masks(lengths_ref, start)
        for low, high in widths:
            columns = slice(low, high)
            seen = window_before(proj_ref, start, columns)
            summed = seen[8:] * filter_ref[CONV - 1 : CONV, columns]
            for offset in range(1, CONV):
                tap = CONV - 1 - offset
                mask = (since >= offset).astype(jnp.float32)
                summed = summed + seen[8 - offset : 8 - offset + BLOCK] * (
                    mask * filter_ref[tap : tap + 1, columns]
                )
            act_ref[rows, columns] = summed
        tail_tile = proj_ref[rows, tail_at : tail_at + TAIL]
        rate, _ = decays(tail_tile, decay_ref[0:1, :], decay_ref[1:2, :])
        beta_tile = sigmoid(tail_tile)
        cumulative = mm_sum(lower_ones(), rate)
        flipped = cumulative.T
        lowers, kept = [], []
        for head in range(heads):
            key_cols = slice(head * KH, (head + 1) * KH)
            within, initial, tail, end = head_decay(
                cumulative, flipped, head, linked, carried, tail_mask, last_carried
            )
            beta = beta_tile[:, heads + head : heads + head + 1]
            summed = act_ref[rows, key_cols]
            query = summed * sigmoid(summed)
            summed = act_ref[rows, key_dim + head * KH : key_dim + (head + 1) * KH]
            key = summed * sigmoid(summed)
            key = key * lax.rsqrt(jnp.sum(key * key, axis=-1, keepdims=True) + epsilon)
            summed = act_ref[rows, 2 * key_dim + head * VH : 2 * key_dim + (head + 1) * VH]
            value = summed * sigmoid(summed)
            both = mm_gram(jnp.concatenate([key, query], axis=0), key, NT)
            gram = both[:BLOCK] * jnp.where(strict, within, 0.0)
            score = both[BLOCK:] * within
            lowers.append(beta * gram)
            kept.append((query * initial, key, value, beta, initial, tail, end, score))
            at = pl.ds(pl.multiple_of((block * heads + head) * BLOCK, BLOCK), BLOCK)
            gram_ref[at, :] = gram
            score_ref[at, :] = score
        inverses = unit_inverses(lowers)
        row = lax.broadcasted_iota(jnp.int32, (KH, KH), 0)
        column = lax.broadcasted_iota(jnp.int32, (KH, KH), 1)
        for head in range(heads):
            query, key, value, beta, initial, tail, end, score = kept[head]
            at = pl.ds(pl.multiple_of((block * heads + head) * BLOCK, BLOCK), BLOCK)
            key_cols = slice(head * KH, (head + 1) * KH)
            value_cols = slice(head * VH, (head + 1) * VH)
            inverse_ref[at, :] = inverses[head]
            pseudo = mm_out(inverses[head], beta * value)
            correct = mm_out(inverses[head], (beta * initial) * key)
            tail_key = tail * key
            step = jnp.where(row == column, end, 0.0) - mm_chain(tail_key, correct, TN)
            pseudo_ref[rows, value_cols] = pseudo
            correct_ref[rows, key_cols] = correct
            step_ref[at, :] = step
            add_ref[at, :] = mm_chain(tail_key, pseudo, TN)
            query_ref[rows, key_cols] = query
        return 0

    lax.fori_loop(0, blocks, first, 0)

    def second(block, states):
        after = []
        for head in range(heads):
            at = pl.ds(pl.multiple_of((block * heads + head) * BLOCK, BLOCK), BLOCK)
            state_ref[at, :] = states[head]
            after.append(mm_chain(step_ref[at, :], states[head]) + add_ref[at, :])
        return tuple(after)

    lax.fori_loop(
        0, blocks, second, tuple(jnp.zeros((KH, VH), jnp.float32) for _ in range(heads))
    )

    def third(block, _):
        start = pl.multiple_of(block * BLOCK, BLOCK)
        rows = pl.ds(start, BLOCK)
        for head in range(heads):
            at = pl.ds(pl.multiple_of((block * heads + head) * BLOCK, BLOCK), BLOCK)
            key_cols = slice(head * KH, (head + 1) * KH)
            value_cols = slice(head * VH, (head + 1) * VH)
            state = state_ref[at, :]
            score = score_ref[at, :]
            correct = correct_ref[rows, key_cols]
            query = query_ref[rows, key_cols]
            delta = pseudo_ref[rows, value_cols] - mm_out(correct, state)
            result = mm_out(query, state) + mm_out(score, delta)
            delta_ref[rows, value_cols] = delta
            result_ref[rows, value_cols] = result
            query_ref[rows, key_cols] = query - mm_out(score, correct)
            gate = proj_ref[
                rows, 2 * key_dim + value_dim + head * VH : 2 * key_dim + value_dim + (head + 1) * VH
            ]
            scale = lax.rsqrt(jnp.mean(result * result, axis=-1, keepdims=True) + out_epsilon)
            mixed = result * scale * gain_ref[...] * (gate * sigmoid(gate))
            mixed_ref[rows, value_cols] = mixed.astype(mixed_ref.dtype)
        return 0

    lax.fori_loop(0, blocks, third, 0)


def backward_kernel(
    heads,
    lengths_ref,
    grad_ref,
    proj_ref,
    filter_ref,
    decay_ref,
    gain_ref,
    act_ref,
    inverse_ref,
    state_ref,
    delta_ref,
    result_ref,
    score_ref,
    gram_ref,
    query_ref,
    step_ref,
    out_ref,
    filter_grad_ref,
    decay_grad_ref,
    gain_grad_ref,
    back_ref,
    reach_ref,
    act_grad_ref,
):
    length = proj_ref.shape[0]
    blocks = length // BLOCK
    key_dim, value_dim = heads * KH, heads * VH
    gate_at = 2 * key_dim + value_dim
    tail_at = 2 * key_dim + 2 * value_dim
    filter_grad_ref[...] = jnp.zeros_like(filter_grad_ref)
    decay_grad_ref[...] = jnp.zeros_like(decay_grad_ref)
    gain_grad_ref[...] = jnp.zeros_like(gain_grad_ref)
    act_grad_ref[length : length + 8, :] = jnp.zeros((8, gate_at), jnp.float32)

    def first(block, _):
        start = pl.multiple_of(block * BLOCK, BLOCK)
        rows = pl.ds(start, BLOCK)
        for head in range(heads):
            at = pl.ds(pl.multiple_of((block * heads + head) * BLOCK, BLOCK), BLOCK)
            key_cols = slice(head * KH, (head + 1) * KH)
            value_cols = slice(head * VH, (head + 1) * VH)
            gate_cols = slice(gate_at + head * VH, gate_at + (head + 1) * VH)
            result = result_ref[rows, value_cols]
            gate = proj_ref[rows, gate_cols]
            grad = grad_ref[rows, value_cols]
            sigma = sigmoid(gate)
            scale = lax.rsqrt(jnp.mean(result * result, axis=-1, keepdims=True) + out_epsilon)
            normed = result * scale
            out_ref[rows, gate_cols] = (
                grad * normed * gain_ref[...] * (sigma * (1.0 + gate * (1.0 - sigma)))
            ).astype(out_ref.dtype)
            grad = grad * (gate * sigma)
            gain_grad_ref[0:1, :] += jnp.sum(grad * normed, axis=0, keepdims=True)
            grad = grad * gain_ref[...]
            grad = scale * (grad - normed * jnp.mean(grad * normed, axis=-1, keepdims=True))
            back_ref[rows, value_cols] = grad
            reach_ref[at, :] = mm_chain(query_ref[rows, key_cols], grad, TN)
        return 0

    lax.fori_loop(0, blocks, first, 0)

    def second(index, states):
        block = blocks - 1 - index
        after = []
        for head in range(heads):
            at = pl.ds(pl.multiple_of((block * heads + head) * BLOCK, BLOCK), BLOCK)
            reach = reach_ref[at, :]
            reach_ref[at, :] = states[head]
            after.append(mm_chain(step_ref[at, :], states[head], TN) + reach)
        return tuple(after)

    lax.fori_loop(
        0, blocks, second, tuple(jnp.zeros((KH, VH), jnp.float32) for _ in range(heads))
    )

    def third(block, _):
        start = pl.multiple_of(block * BLOCK, BLOCK)
        rows = pl.ds(start, BLOCK)
        since, linked, strict, carried, tail_mask, last_carried = block_masks(lengths_ref, start)
        tail_tile = proj_ref[rows, tail_at : tail_at + TAIL]
        rate, logits = decays(tail_tile, decay_ref[0:1, :], decay_ref[1:2, :])
        beta_tile = sigmoid(tail_tile)
        cumulative = mm_sum(lower_ones(), rate)
        flipped = cumulative.T
        lane = lax.broadcasted_iota(jnp.int32, (BLOCK, TAIL), 1)
        place = lax.broadcasted_iota(jnp.int32, (BLOCK, TAIL), 0)
        cum_grad = jnp.zeros((BLOCK, TAIL), jnp.float32)
        cum_across = jnp.zeros((TAIL, BLOCK), jnp.float32)
        beta_grad = jnp.zeros((BLOCK, TAIL), jnp.float32)
        for head in range(heads):
            at = pl.ds(pl.multiple_of((block * heads + head) * BLOCK, BLOCK), BLOCK)
            key_cols = slice(head * KH, (head + 1) * KH)
            key_act = slice(key_dim + head * KH, key_dim + (head + 1) * KH)
            value_act = slice(2 * key_dim + head * VH, 2 * key_dim + (head + 1) * VH)
            value_cols = slice(head * VH, (head + 1) * VH)
            within, initial, tail, end = head_decay(
                cumulative, flipped, head, linked, carried, tail_mask, last_carried
            )
            beta = beta_tile[:, heads + head : heads + head + 1]
            summed = act_ref[rows, key_cols]
            query_sigma = sigmoid(summed)
            query = summed * query_sigma
            query_slope = query_sigma * (1.0 + summed * (1.0 - query_sigma))
            summed = act_ref[rows, key_act]
            key_sigma = sigmoid(summed)
            key = summed * key_sigma
            key_slope = key_sigma * (1.0 + summed * (1.0 - key_sigma))
            key_scale = lax.rsqrt(jnp.sum(key * key, axis=-1, keepdims=True) + epsilon)
            key = key * key_scale
            summed = act_ref[rows, value_act]
            value_sigma = sigmoid(summed)
            value = summed * value_sigma
            value_slope = value_sigma * (1.0 + summed * (1.0 - value_sigma))
            grad = back_ref[rows, value_cols]
            after = reach_ref[at, :]
            state = state_ref[at, :]
            score = score_ref[at, :]
            gram = gram_ref[at, :]
            delta = delta_ref[rows, value_cols]
            tail_key = tail * key
            delta_grad = mm_back(score, grad, TN) + mm_back(tail_key, after)
            scaled_grad = mm_back(inverse_ref[at, :], delta_grad, TN)
            pair = jnp.concatenate([grad, scaled_grad], axis=0)
            by_state = mm_back(pair, state, NT)
            query_grad = by_state[:BLOCK]
            written_grad = -by_state[BLOCK:]
            by_delta = mm_back(pair, delta, NT)
            tail_grad = mm_back(delta, after, NT)
            score_grad = by_delta[:BLOCK]
            lower_grad = -by_delta[BLOCK:]
            initial_key = initial * key
            beta_one = (
                jnp.sum(scaled_grad * value, axis=-1, keepdims=True)
                + jnp.sum(written_grad * initial_key, axis=-1, keepdims=True)
                + jnp.sum(lower_grad * gram, axis=-1, keepdims=True)
            )
            spread_grad = score_grad * score + lower_grad * (beta * gram)
            tail_one = tail * jnp.sum(tail_grad * key, axis=-1, keepdims=True)
            initial_one = initial * (
                jnp.sum(query_grad * query, axis=-1, keepdims=True)
                + beta * jnp.sum(written_grad * key, axis=-1, keepdims=True)
            )
            last_one = jnp.sum(tail_one, axis=0, keepdims=True) + end * jnp.sum(
                jnp.sum(state * after, axis=-1, keepdims=True), axis=0, keepdims=True
            )
            cum_one = jnp.sum(spread_grad, axis=-1, keepdims=True) + initial_one - tail_one
            cum_grad = cum_grad + jnp.where(lane == head, cum_one, 0.0)
            cum_grad = cum_grad + jnp.where((lane == head) & (place == BLOCK - 1), last_one, 0.0)
            cum_across = cum_across + jnp.where(
                place == head, jnp.sum(spread_grad, axis=0, keepdims=True), 0.0
            )
            beta_grad = beta_grad + jnp.where(lane == heads + head, beta_one, 0.0)
            score_grad = score_grad * within
            gram_grad = jnp.where(strict, lower_grad * within, 0.0) * beta
            by_key = mm_back(jnp.concatenate([score_grad, gram_grad], axis=0), key)
            query_grad = initial * query_grad + by_key[:BLOCK]
            key_grad = (
                (beta * initial) * written_grad
                + tail * tail_grad
                + by_key[BLOCK:]
                + mm_back(gram_grad, key, TN)
                + mm_back(score_grad, query, TN)
            )
            key_grad = key_scale * (
                key_grad - key * jnp.sum(key_grad * key, axis=-1, keepdims=True)
            )
            act_grad_ref[rows, key_cols] = query_grad * query_slope
            act_grad_ref[rows, key_act] = key_grad * key_slope
            act_grad_ref[rows, value_act] = (beta * scaled_grad) * value_slope
        cum_grad = cum_grad - cum_across.T
        rate_grad = mm_sum(lower_ones(), cum_grad, TN)
        logit_grad = rate_grad * (-jnp.exp(decay_ref[0:1, :])) * sigmoid(logits)
        decay_grad_ref[0:1, :] += jnp.sum(rate_grad * rate, axis=0, keepdims=True)
        decay_grad_ref[1:2, :] += jnp.sum(logit_grad, axis=0, keepdims=True)
        out_ref[rows, tail_at : tail_at + TAIL] = jnp.where(
            lane < heads, logit_grad, beta_grad * beta_tile * (1.0 - beta_tile)
        ).astype(out_ref.dtype)
        return 0

    lax.fori_loop(0, blocks, third, 0)

    def fourth(block, _):
        start = pl.multiple_of(block * BLOCK, BLOCK)
        rows = pl.ds(start, BLOCK)
        positions = start + lax.broadcasted_iota(jnp.int32, (BLOCK + 8, 1), 0)
        since = positions - document_starts(lengths_ref, positions)
        for low, high in (
            (0, key_dim),
            (key_dim, 2 * key_dim),
            (2 * key_dim, 2 * key_dim + value_dim),
        ):
            columns = slice(low, high)
            later = jnp.concatenate(
                [
                    act_grad_ref[rows, columns],
                    act_grad_ref[pl.ds(pl.multiple_of(start + BLOCK, 8), 8), columns],
                ],
                axis=0,
            )
            seen = window_before(proj_ref, start, columns)
            here = later[:BLOCK]
            summed = here * filter_ref[CONV - 1 : CONV, columns]
            filter_grad_ref[CONV - 1 : CONV, columns] += jnp.sum(
                here * seen[8:], axis=0, keepdims=True
            )
            for offset in range(1, CONV):
                tap = CONV - 1 - offset
                mask = (since >= offset).astype(jnp.float32)
                summed = summed + later[offset : offset + BLOCK] * (
                    mask[offset : offset + BLOCK] * filter_ref[tap : tap + 1, columns]
                )
                filter_grad_ref[tap : tap + 1, columns] += jnp.sum(
                    here * (mask[:BLOCK] * seen[8 - offset : 8 - offset + BLOCK]),
                    axis=0,
                    keepdims=True,
                )
            out_ref[rows, columns] = summed.astype(out_ref.dtype)
        return 0

    lax.fori_loop(0, blocks, fourth, 0)


def f32(*shape):
    return jax.ShapeDtypeStruct(shape, jnp.float32)


VMEM = pl.BlockSpec(memory_space=pltpu.VMEM)
SMEM = pl.BlockSpec(memory_space=pltpu.SMEM)
PARAMS = pltpu.CompilerParams(vmem_limit_bytes=60 * 2**20)


def mixer_forward(lengths, proj, filters, decay_pair, out_gain, heads):
    length = proj.shape[0]
    pairs = length // BLOCK * heads * BLOCK
    key_dim, value_dim = heads * KH, heads * VH
    return pl.pallas_call(
        functools.partial(forward_kernel, heads),
        out_shape=(
            jax.ShapeDtypeStruct((length, value_dim), jnp.bfloat16),
            f32(length, 2 * key_dim + value_dim),
            f32(pairs, BLOCK),
            f32(pairs, VH),
            f32(length, value_dim),
            f32(length, value_dim),
            f32(pairs, BLOCK),
            f32(pairs, BLOCK),
            f32(length, key_dim),
            f32(pairs, KH),
        ),
        in_specs=[SMEM] + [VMEM] * 4,
        out_specs=(VMEM,) * 10,
        scratch_shapes=[
            pltpu.VMEM((length, value_dim), jnp.float32),
            pltpu.VMEM((length, key_dim), jnp.float32),
            pltpu.VMEM((pairs, VH), jnp.float32),
        ],
        compiler_params=PARAMS,
        cost_estimate=pl.CostEstimate(
            flops=30 * 10**9, bytes_accessed=24 * 2**20, transcendentals=0
        ),
        name="mixer_forward",
    )(lengths, proj, filters, decay_pair, out_gain)


def mixer_backward(lengths, grad, proj, filters, decay_pair, out_gain, kept, heads):
    length = proj.shape[0]
    pairs = length // BLOCK * heads * BLOCK
    key_dim, value_dim = heads * KH, heads * VH
    return pl.pallas_call(
        functools.partial(backward_kernel, heads),
        out_shape=(
            jax.ShapeDtypeStruct(proj.shape, jnp.bfloat16),
            f32(CONV, 2 * key_dim + value_dim),
            f32(8, TAIL),
            f32(8, VH),
        ),
        in_specs=[SMEM] + [VMEM] * (5 + len(kept)),
        out_specs=(VMEM,) * 4,
        scratch_shapes=[
            pltpu.VMEM((length, value_dim), jnp.float32),
            pltpu.VMEM((pairs, VH), jnp.float32),
            pltpu.VMEM((length + 8, 2 * key_dim + value_dim), jnp.float32),
        ],
        compiler_params=PARAMS,
        cost_estimate=pl.CostEstimate(
            flops=30 * 10**9, bytes_accessed=32 * 2**20, transcendentals=0
        ),
        name="mixer_backward",
    )(lengths, grad, proj, filters, decay_pair, out_gain, *kept)


def plain_product(first_mat, second_mat):
    return jnp.dot(first_mat, second_mat, preferred_element_type=jnp.float32)


def left_product(first_mat, second_mat):
    return lax.dot_general(first_mat, second_mat, TN, preferred_element_type=jnp.float32)


def right_product(first_mat, second_mat):
    return lax.dot_general(first_mat, second_mat, NT, preferred_element_type=jnp.float32)


def rms_scale(values, scales):
    return values * lax.rsqrt(jnp.mean(values * values, axis=-1, keepdims=True) + epsilon) * scales


def norm_back(inputs, scales, grad_normed):
    inverse = lax.rsqrt(jnp.mean(inputs * inputs, axis=-1, keepdims=True) + epsilon)
    weighted = scales * grad_normed
    grad_inputs = inverse * weighted - inputs * (inverse * inverse * inverse) * jnp.mean(
        weighted * inputs, axis=-1, keepdims=True
    )
    grad_scales = jnp.sum(grad_normed * inputs * inverse, axis=0)
    return (grad_inputs, grad_scales)


def swap(values, axis):
    return lax.ppermute(values, axis, [(0, 1), (1, 0)])


def joined(own, other, axis):
    leads = lax.axis_index(axis) == 0
    return jnp.concatenate(
        [jnp.where(leads, own, other), jnp.where(leads, other, own)], axis=1
    )


def gather_features(own):
    half = joined(own, swap(own, "col"), "col")
    return joined(half, swap(half, "row"), "row")


def half_of(values, index):
    width = values.shape[1] // 2
    return lax.dynamic_slice_in_dim(values, index * width, width, 1)


def scatter_features(partial):
    for axis in ("row", "col"):
        index = lax.axis_index(axis)
        other = swap(half_of(partial, 1 - index).astype(jnp.bfloat16), axis)
        partial = half_of(partial, index) + other.astype(jnp.float32)
    return partial


def body(
    tokens,
    cotangent,
    lengths,
    norm_gain,
    w_query,
    w_key,
    w_value,
    w_alpha,
    w_beta,
    conv_query,
    conv_key,
    conv_value,
    decay_log,
    decay_bias,
    w_outgate,
    out_gain,
    w_out,
    ffn_gain,
    w_gate,
    w_up,
    w_down,
):
    heads = w_alpha.shape[1]
    key_dim, value_dim = heads * KH, heads * VH
    small = jnp.zeros((w_alpha.shape[0], TAIL - 2 * heads), w_alpha.dtype)
    weights = jnp.concatenate([w_query, w_key, w_value, w_outgate, w_alpha, w_beta, small], axis=1)
    filters = jnp.concatenate([conv_query, conv_key, conv_value], axis=1)
    decay_pair = jnp.pad(jnp.stack([decay_log, decay_bias]), ((0, 6), (0, TAIL - heads)))
    gain_row = out_gain[None]

    whole = gather_features(tokens).astype(jnp.float32)
    grad_out = gather_features(cotangent)
    normed = rms_scale(whole, norm_gain).astype(jnp.bfloat16)
    proj = plain_product(normed, weights)
    mixed, *kept = mixer_forward(lengths, proj, filters, decay_pair, gain_row, heads)
    hidden_own = tokens.astype(jnp.float32) + scatter_features(plain_product(mixed, w_out))
    hidden = gather_features(hidden_own)
    normed_ffn = rms_scale(hidden, ffn_gain).astype(jnp.bfloat16)
    gate_act = plain_product(normed_ffn, w_gate)
    up_act = plain_product(normed_ffn, w_up)
    sigma = jax.nn.sigmoid(gate_act)
    product = (gate_act * sigma * up_act).astype(jnp.bfloat16)
    grad_product = right_product(grad_out, w_down)
    grad_gate_act = (grad_product * up_act * sigma * (1.0 + gate_act * (1.0 - sigma))).astype(
        jnp.bfloat16
    )
    grad_up_act = (grad_product * gate_act * sigma).astype(jnp.bfloat16)
    grad_normed_ffn = right_product(grad_gate_act, w_gate) + right_product(grad_up_act, w_up)
    grad_hidden_part, grad_ffn_gain = norm_back(hidden, ffn_gain, grad_normed_ffn)
    grad_down = left_product(product, grad_out)
    grad_gate = left_product(normed_ffn, grad_gate_act)
    grad_up = left_product(normed_ffn, grad_up_act)
    ffn_sums = lax.psum(
        tuple(item.astype(jnp.bfloat16) for item in (grad_down, grad_gate, grad_up)), "dp"
    )
    grad_hidden_own = (
        cotangent.astype(jnp.float32) + scatter_features(grad_hidden_part)
    ).astype(jnp.bfloat16)
    grad_hidden = gather_features(grad_hidden_own)
    output = (hidden_own + scatter_features(plain_product(product, w_down))).astype(jnp.bfloat16)
    grad_mixed = right_product(grad_hidden, w_out)
    grad_proj, filter_grad, decay_grad, gain_grad = mixer_backward(
        lengths, grad_mixed, proj, filters, decay_pair, gain_row, tuple(kept), heads
    )
    grad_normed = right_product(grad_proj, weights)
    grad_input_part, grad_norm_gain = norm_back(whole, norm_gain, grad_normed)
    grad_out_proj = left_product(mixed, grad_hidden)
    grad_weights = left_product(normed, grad_proj)
    tail_at = 2 * key_dim + 2 * value_dim
    mixer_sums = lax.psum(
        (
            grad_out_proj.astype(jnp.bfloat16),
            grad_weights[:, :tail_at].astype(jnp.bfloat16),
        ),
        "dp",
    )
    input_grad = (
        grad_hidden_own.astype(jnp.float32) + scatter_features(grad_input_part)
    ).astype(jnp.bfloat16)
    gains = lax.psum(
        jnp.concatenate([grad_norm_gain, grad_ffn_gain, gain_grad[0]]), ("row", "col")
    )
    sizes = (
        gains,
        filter_grad.reshape(-1),
        grad_weights[:, tail_at : tail_at + 2 * heads].reshape(-1),
        decay_grad[:2, :heads].reshape(-1),
    )
    small_sum = lax.psum(jnp.concatenate(sizes), "dp")
    width = norm_gain.shape[0]
    places = [0]
    for item in sizes:
        places.append(places[-1] + item.shape[0])
    pieces = [small_sum[low:high] for low, high in zip(places, places[1:])]
    filter_sum = pieces[1].reshape(filters.shape)
    pair_sum = pieces[2].reshape(-1, 2 * heads)
    decay_sum = pieces[3].reshape(2, heads)
    down_sum, gate_sum, up_sum = (item.astype(jnp.float32) for item in ffn_sums)
    out_sum, weight_sum = (item.astype(jnp.float32) for item in mixer_sums)
    return (
        output,
        input_grad,
        pieces[0][:width],
        weight_sum[:, :key_dim],
        weight_sum[:, key_dim : 2 * key_dim],
        weight_sum[:, 2 * key_dim : 2 * key_dim + value_dim],
        pair_sum[:, :heads],
        pair_sum[:, heads:],
        filter_sum[:, :key_dim],
        filter_sum[:, key_dim : 2 * key_dim],
        filter_sum[:, 2 * key_dim :],
        decay_sum[0],
        decay_sum[1],
        weight_sum[:, 2 * key_dim + value_dim :],
        pieces[0][2 * width :],
        out_sum,
        pieces[0][width : 2 * width],
        gate_sum,
        up_sum,
        down_sum,
    )


def solution(mesh):
    placed = (
        P("dp", ("row", "col")),
        P("dp", ("row", "col")),
        P("dp", None),
        P(),
        P(None, ("row", "col")),
        P(None, ("row", "col")),
        P(None, ("row", "col")),
        P(None, ("row", "col")),
        P(None, ("row", "col")),
        P(None, ("row", "col")),
        P(None, ("row", "col")),
        P(None, ("row", "col")),
        P(("row", "col")),
        P(("row", "col")),
        P(None, ("row", "col")),
        P(),
        P(("row", "col"), None),
        P(),
        P(None, ("row", "col")),
        P(None, ("row", "col")),
        P(("row", "col"), None),
    )
    return jax.shard_map(
        body,
        mesh=mesh,
        in_specs=placed,
        out_specs=(
            P("dp", ("row", "col")),
            P("dp", ("row", "col")),
            P(),
            P(None, ("row", "col")),
            P(None, ("row", "col")),
            P(None, ("row", "col")),
            P(None, ("row", "col")),
            P(None, ("row", "col")),
            P(None, ("row", "col")),
            P(None, ("row", "col")),
            P(None, ("row", "col")),
            P(("row", "col")),
            P(("row", "col")),
            P(None, ("row", "col")),
            P(),
            P(("row", "col"), None),
            P(),
            P(None, ("row", "col")),
            P(None, ("row", "col")),
            P(("row", "col"), None),
        ),
        check_vma=False,
    )
```

```python
import functools

import jax
import jax.numpy as jnp
from jax import lax
from jax.experimental import pallas as pl
from jax.experimental.pallas import tpu as pltpu
from jax.sharding import PartitionSpec as P

KH = 128
VH = 256
CONV = 4
BLOCK = 128
TAIL = 128
GROUP = 4

epsilon = 1e-06
out_epsilon = 0.05

NN = (((1,), (0,)), ((), ()))
NT = (((1,), (1,)), ((), ()))
TN = (((0,), (0,)), ((), ()))


def product_one(first, second, dims=NN):
    return lax.dot_general(
        first.astype(jnp.bfloat16),
        second.astype(jnp.bfloat16),
        dims,
        preferred_element_type=jnp.float32,
    )


def product_three(first, second, dims=NN):
    (along_first,), (along_second,) = dims[0]
    across = 1 - along_second
    first_high = first.astype(jnp.bfloat16)
    second_high = second.astype(jnp.bfloat16)
    first_low = (first - first_high.astype(jnp.float32)).astype(jnp.bfloat16)
    second_low = (second - second_high.astype(jnp.float32)).astype(jnp.bfloat16)
    dot = functools.partial(
        lax.dot_general, dimension_numbers=dims, preferred_element_type=jnp.float32
    )
    short = first.shape[along_first] <= 128
    narrow = second.shape[across] <= 128
    count = second.shape[across]
    if short:
        stacked = jnp.concatenate([first_high, first_low], axis=along_first)
    if short and narrow:
        over = jnp.concatenate([second_high, second_low], axis=across)
        under = jnp.concatenate([second_high, jnp.zeros_like(second_low)], axis=across)
        both = dot(stacked, jnp.concatenate([over, under], axis=along_second))
        return both[:, :count] + both[:, count:]
    if short:
        twice = jnp.concatenate([second_high, second_high], axis=along_second)
        return dot(stacked, twice) + dot(first_high, second_low)
    if narrow:
        both = dot(first_high, jnp.concatenate([second_high, second_low], axis=across))
        return both[:, :count] + (both[:, count:] + dot(first_low, second_high))
    return dot(first_high, second_high) + (
        dot(first_high, second_low) + dot(first_low, second_high)
    )


def product_six(first, second, dims=NN):
    return lax.dot_general(
        first, second, dims, precision=lax.Precision.HIGHEST, preferred_element_type=jnp.float32
    )


mm_sum = product_six
mm_inverse = product_three
mm_chain = product_three
mm_gram = product_three
mm_out = product_three
mm_back = product_three


def sigmoid(values):
    return 1.0 / (1.0 + jnp.exp(-values))


def softplus(values):
    return jnp.maximum(values, 0.0) + jnp.log1p(jnp.exp(-jnp.abs(values)))


def document_starts(lengths_ref, positions):
    starts = jnp.zeros_like(positions)
    end = 0
    for doc in range(lengths_ref.shape[1] - 1):
        end = end + lengths_ref[0, doc]
        starts = jnp.where(positions >= end, end, starts)
    return starts


def start_of(lengths_ref, position):
    start = 0
    end = 0
    for doc in range(lengths_ref.shape[1] - 1):
        end = end + lengths_ref[0, doc]
        start = jnp.where(position >= end, end, start)
    return start


def unit_inverses(lowers):
    size = lowers[0].shape[0]
    row = lax.broadcasted_iota(jnp.int32, (size, size), 0)
    column = lax.broadcasted_iota(jnp.int32, (size, size), 1)
    eye = (row == column).astype(jnp.float32)
    within = (row >> 3) == (column >> 3)
    inner = [jnp.where(within, low, 0.0) for low in lowers]
    square = [mm_inverse(one, one) for one in inner]
    cube = [mm_inverse(one, two) for one, two in zip(inner, square)]
    fourth = [mm_inverse(two, two) for two in square]
    part = [eye - one + two - three for one, two, three in zip(inner, square, cube)]
    result = [one + mm_inverse(one, four) for one, four in zip(part, fourth)]
    shift = 3
    while (1 << shift) < size:
        off = ((row >> (shift + 1)) == (column >> (shift + 1))) & (
            (row >> shift) != (column >> shift)
        )
        edge = [mm_inverse(jnp.where(off, low, 0.0), one) for low, one in zip(lowers, result)]
        result = [one - mm_inverse(one, two) for one, two in zip(result, edge)]
        shift += 1
    return result


def window_before(ref, start, columns):
    early = pl.multiple_of(jnp.maximum(start - 8, 0), 8)
    return jnp.concatenate(
        [ref[pl.ds(early, 8), columns], ref[pl.ds(start, BLOCK), columns]], axis=0
    )


def decays(tail, scales, biases):
    logits = tail + biases
    return -jnp.exp(scales) * softplus(logits), logits


def block_masks(lengths_ref, start):
    positions = start + lax.broadcasted_iota(jnp.int32, (BLOCK, 1), 0)
    starts = document_starts(lengths_ref, positions)
    columns = start + lax.broadcasted_iota(jnp.int32, (BLOCK, BLOCK), 1)
    rows = start + lax.broadcasted_iota(jnp.int32, (BLOCK, BLOCK), 0)
    linked = (starts <= columns) & (rows >= columns)
    strict = rows > columns
    carried = (starts < start).astype(jnp.float32)
    last_start = start_of(lengths_ref, start + BLOCK - 1)
    tail_mask = (positions >= last_start).astype(jnp.float32)
    last_carried = (last_start < start).astype(jnp.float32)
    return positions - starts, linked, strict, carried, tail_mask, last_carried


def lower_ones():
    row = lax.broadcasted_iota(jnp.int32, (BLOCK, BLOCK), 0)
    column = lax.broadcasted_iota(jnp.int32, (BLOCK, BLOCK), 1)
    return (row >= column).astype(jnp.float32)


def head_decay(cumulative, flipped, head, linked, carried, tail_mask, last_carried):
    cum = cumulative[:, head : head + 1]
    spread = cum - flipped[head : head + 1, :]
    within = jnp.where(linked, jnp.exp(jnp.where(linked, spread, 0.0)), 0.0)
    last = cumulative[BLOCK - 1 : BLOCK, head : head + 1]
    initial = jnp.exp(cum) * carried
    tail = jnp.exp(last - cum) * tail_mask
    end = jnp.exp(last) * last_carried
    return within, initial, tail, end


def forward_kernel(
    heads,
    lengths_ref,
    proj_ref,
    gate_ref,
    filter_ref,
    decay_ref,
    gain_ref,
    mixed_ref,
    act_ref,
    inverse_ref,
    state_ref,
    delta_ref,
    result_ref,
    score_ref,
    gram_ref,
    query_ref,
    step_ref,
    pseudo_ref,
    correct_ref,
    add_ref,
):
    length = proj_ref.shape[0]
    blocks = length // BLOCK
    key_dim, value_dim = heads * KH, heads * VH
    tail_at = 2 * key_dim + value_dim
    widths = ((0, key_dim), (key_dim, 2 * key_dim), (2 * key_dim, 2 * key_dim + value_dim))

    def first(turn, _):
        lowers, kept = [], []
        for lane in range(GROUP):
            block = turn * GROUP + lane
            start = pl.multiple_of(block * BLOCK, BLOCK)
            rows = pl.ds(start, BLOCK)
            since, linked, strict, carried, tail_mask, last_carried = block_masks(
                lengths_ref, start
            )
            parts = []
            for low, high in widths:
                columns = slice(low, high)
                seen = window_before(proj_ref, start, columns)
                summed = seen[8:] * filter_ref[CONV - 1 : CONV, columns]
                for offset in range(1, CONV):
                    tap = CONV - 1 - offset
                    mask = (since >= offset).astype(jnp.float32)
                    summed = summed + seen[8 - offset : 8 - offset + BLOCK] * (
                        mask * filter_ref[tap : tap + 1, columns]
                    )
                act_ref[rows, columns] = summed
                parts.append(summed * sigmoid(summed))
            tail_tile = proj_ref[rows, tail_at : tail_at + TAIL]
            rate, _ = decays(tail_tile, decay_ref[0:1, :], decay_ref[1:2, :])
            beta_tile = sigmoid(tail_tile)
            cumulative = mm_sum(lower_ones(), rate)
            flipped = cumulative.T
            for head in range(heads):
                within, initial, tail, end = head_decay(
                    cumulative, flipped, head, linked, carried, tail_mask, last_carried
                )
                beta = beta_tile[:, heads + head : heads + head + 1]
                query = parts[0][:, head * KH : (head + 1) * KH]
                key = parts[1][:, head * KH : (head + 1) * KH]
                key = key * lax.rsqrt(jnp.sum(key * key, axis=-1, keepdims=True) + epsilon)
                value = parts[2][:, head * VH : (head + 1) * VH]
                both = mm_gram(jnp.concatenate([key, query], axis=0), key, NT)
                gram = both[:BLOCK] * jnp.where(strict, within, 0.0)
                score = both[BLOCK:] * within
                lowers.append(beta * gram)
                at = pl.ds(pl.multiple_of((block * heads + head) * BLOCK, BLOCK), BLOCK)
                gram_ref[at, :] = gram
                score_ref[at, :] = score
                query_ref[rows, head * KH : (head + 1) * KH] = query * initial
                kept.append((rows, at, head, key, value, beta, initial, tail, end))
        inverses = unit_inverses(lowers)
        row = lax.broadcasted_iota(jnp.int32, (KH, KH), 0)
        column = lax.broadcasted_iota(jnp.int32, (KH, KH), 1)
        solved = []
        for inverse, (rows, at, head, key, value, beta, initial, tail, end) in zip(inverses, kept):
            inverse_ref[at, :] = inverse
            pseudo = mm_out(inverse, beta * value)
            correct = mm_out(inverse, (beta * initial) * key)
            solved.append((pseudo, correct))
        for (pseudo, correct), (rows, at, head, key, value, beta, initial, tail, end) in zip(
            solved, kept
        ):
            tail_key = tail * key
            step = jnp.where(row == column, end, 0.0) - mm_chain(tail_key, correct, TN)
            pseudo_ref[rows, head * VH : (head + 1) * VH] = pseudo
            correct_ref[rows, head * KH : (head + 1) * KH] = correct
            step_ref[at, :] = step
            add_ref[at, :] = mm_chain(tail_key, pseudo, TN)
        return 0

    lax.fori_loop(0, blocks // GROUP, first, 0)

    def second(block, states):
        after = []
        for head in range(heads):
            at = pl.ds(pl.multiple_of((block * heads + head) * BLOCK, BLOCK), BLOCK)
            state_ref[at, :] = states[head]
            after.append(mm_chain(step_ref[at, :], states[head]) + add_ref[at, :])
        return tuple(after)

    lax.fori_loop(
        0, blocks, second, tuple(jnp.zeros((KH, VH), jnp.float32) for _ in range(heads))
    )

    def third(block, _):
        start = pl.multiple_of(block * BLOCK, BLOCK)
        rows = pl.ds(start, BLOCK)
        for head in range(heads):
            at = pl.ds(pl.multiple_of((block * heads + head) * BLOCK, BLOCK), BLOCK)
            key_cols = slice(head * KH, (head + 1) * KH)
            value_cols = slice(head * VH, (head + 1) * VH)
            state = state_ref[at, :]
            score = score_ref[at, :]
            correct = correct_ref[rows, key_cols]
            query = query_ref[rows, key_cols]
            delta = pseudo_ref[rows, value_cols] - mm_out(correct, state)
            result = mm_out(query, state) + mm_out(score, delta)
            delta_ref[rows, value_cols] = delta
            result_ref[rows, value_cols] = result
            query_ref[rows, key_cols] = query - mm_out(score, correct)
            gate = gate_ref[rows, value_cols]
            scale = lax.rsqrt(jnp.mean(result * result, axis=-1, keepdims=True) + out_epsilon)
            mixed = result * scale * gain_ref[...] * (gate * sigmoid(gate))
            mixed_ref[rows, value_cols] = mixed.astype(mixed_ref.dtype)
        return 0

    lax.fori_loop(0, blocks, third, 0, unroll=4)


def gate_back_kernel(
    heads,
    grad_ref,
    gate_ref,
    gain_ref,
    result_ref,
    query_ref,
    step_ref,
    out_ref,
    gain_grad_ref,
    back_ref,
    reach_ref,
):
    length = gate_ref.shape[0]
    blocks = length // BLOCK
    gain_grad_ref[...] = jnp.zeros_like(gain_grad_ref)

    def first(block, _):
        start = pl.multiple_of(block * BLOCK, BLOCK)
        rows = pl.ds(start, BLOCK)
        for head in range(heads):
            at = pl.ds(pl.multiple_of((block * heads + head) * BLOCK, BLOCK), BLOCK)
            key_cols = slice(head * KH, (head + 1) * KH)
            value_cols = slice(head * VH, (head + 1) * VH)
            result = result_ref[rows, value_cols]
            gate = gate_ref[rows, value_cols]
            grad = grad_ref[rows, value_cols]
            sigma = sigmoid(gate)
            scale = lax.rsqrt(jnp.mean(result * result, axis=-1, keepdims=True) + out_epsilon)
            normed = result * scale
            out_ref[rows, value_cols] = (
                grad * normed * gain_ref[...] * (sigma * (1.0 + gate * (1.0 - sigma)))
            ).astype(out_ref.dtype)
            grad = grad * (gate * sigma)
            gain_grad_ref[0:1, :] += jnp.sum(grad * normed, axis=0, keepdims=True)
            grad = grad * gain_ref[...]
            grad = scale * (grad - normed * jnp.mean(grad * normed, axis=-1, keepdims=True))
            back_ref[rows, value_cols] = grad
            reach_ref[at, :] = mm_chain(query_ref[rows, key_cols], grad, TN)
        return 0

    lax.fori_loop(0, blocks, first, 0, unroll=4)

    def second(index, states):
        block = blocks - 1 - index
        after = []
        for head in range(heads):
            at = pl.ds(pl.multiple_of((block * heads + head) * BLOCK, BLOCK), BLOCK)
            reach = reach_ref[at, :]
            reach_ref[at, :] = states[head]
            after.append(mm_chain(step_ref[at, :], states[head], TN) + reach)
        return tuple(after)

    lax.fori_loop(
        0, blocks, second, tuple(jnp.zeros((KH, VH), jnp.float32) for _ in range(heads))
    )

def rule_back_kernel(
    heads,
    lengths_ref,
    proj_ref,
    filter_ref,
    decay_ref,
    act_ref,
    inverse_ref,
    state_ref,
    delta_ref,
    score_ref,
    gram_ref,
    back_ref,
    reach_ref,
    out_ref,
    filter_grad_ref,
    decay_grad_ref,
    act_grad_ref,
):
    length = proj_ref.shape[0]
    blocks = length // BLOCK
    key_dim, value_dim = heads * KH, heads * VH
    conv_dim = 2 * key_dim + value_dim
    tail_at = conv_dim

    @pl.when(pl.program_id(0) == 0)
    def _():
        filter_grad_ref[...] = jnp.zeros_like(filter_grad_ref)
        decay_grad_ref[...] = jnp.zeros_like(decay_grad_ref)
        act_grad_ref[length : length + 8, :] = jnp.zeros((8, conv_dim), jnp.float32)

    def third(block, _):
        start = pl.multiple_of(block * BLOCK, BLOCK)
        rows = pl.ds(start, BLOCK)
        since, linked, strict, carried, tail_mask, last_carried = block_masks(lengths_ref, start)
        tail_tile = proj_ref[rows, tail_at : tail_at + TAIL]
        rate, logits = decays(tail_tile, decay_ref[0:1, :], decay_ref[1:2, :])
        beta_tile = sigmoid(tail_tile)
        cumulative = mm_sum(lower_ones(), rate)
        flipped = cumulative.T
        lane = lax.broadcasted_iota(jnp.int32, (BLOCK, TAIL), 1)
        place = lax.broadcasted_iota(jnp.int32, (BLOCK, TAIL), 0)
        cum_grad = jnp.zeros((BLOCK, TAIL), jnp.float32)
        cum_across = jnp.zeros((TAIL, BLOCK), jnp.float32)
        beta_grad = jnp.zeros((BLOCK, TAIL), jnp.float32)
        for head in range(heads):
            at = slice(head * BLOCK, (head + 1) * BLOCK)
            key_cols = slice(head * KH, (head + 1) * KH)
            key_act = slice(key_dim + head * KH, key_dim + (head + 1) * KH)
            value_act = slice(2 * key_dim + head * VH, 2 * key_dim + (head + 1) * VH)
            value_cols = slice(head * VH, (head + 1) * VH)
            within, initial, tail, end = head_decay(
                cumulative, flipped, head, linked, carried, tail_mask, last_carried
            )
            beta = beta_tile[:, heads + head : heads + head + 1]
            summed = act_ref[:, key_cols]
            query_sigma = sigmoid(summed)
            query = summed * query_sigma
            query_slope = query_sigma * (1.0 + summed * (1.0 - query_sigma))
            summed = act_ref[:, key_act]
            key_sigma = sigmoid(summed)
            key = summed * key_sigma
            key_slope = key_sigma * (1.0 + summed * (1.0 - key_sigma))
            key_scale = lax.rsqrt(jnp.sum(key * key, axis=-1, keepdims=True) + epsilon)
            key = key * key_scale
            summed = act_ref[:, value_act]
            value_sigma = sigmoid(summed)
            value = summed * value_sigma
            value_slope = value_sigma * (1.0 + summed * (1.0 - value_sigma))
            grad = back_ref[:, value_cols]
            after = reach_ref[at, :]
            state = state_ref[at, :]
            score = score_ref[at, :]
            gram = gram_ref[at, :]
            delta = delta_ref[:, value_cols]
            tail_key = tail * key
            delta_grad = mm_back(score, grad, TN) + mm_back(tail_key, after)
            scaled_grad = mm_back(inverse_ref[at, :], delta_grad, TN)
            pair = jnp.concatenate([grad, scaled_grad], axis=0)
            by_state = mm_back(pair, state, NT)
            query_grad = by_state[:BLOCK]
            written_grad = -by_state[BLOCK:]
            by_delta = mm_back(pair, delta, NT)
            tail_grad = mm_back(delta, after, NT)
            score_grad = by_delta[:BLOCK]
            lower_grad = -by_delta[BLOCK:]
            initial_key = initial * key
            beta_one = (
                jnp.sum(scaled_grad * value, axis=-1, keepdims=True)
                + jnp.sum(written_grad * initial_key, axis=-1, keepdims=True)
                + jnp.sum(lower_grad * gram, axis=-1, keepdims=True)
            )
            spread_grad = score_grad * score + lower_grad * (beta * gram)
            tail_one = tail * jnp.sum(tail_grad * key, axis=-1, keepdims=True)
            initial_one = initial * (
                jnp.sum(query_grad * query, axis=-1, keepdims=True)
                + beta * jnp.sum(written_grad * key, axis=-1, keepdims=True)
            )
            last_one = jnp.sum(tail_one, axis=0, keepdims=True) + end * jnp.sum(
                jnp.sum(state * after, axis=-1, keepdims=True), axis=0, keepdims=True
            )
            cum_one = jnp.sum(spread_grad, axis=-1, keepdims=True) + initial_one - tail_one
            cum_grad = cum_grad + jnp.where(lane == head, cum_one, 0.0)
            cum_grad = cum_grad + jnp.where((lane == head) & (place == BLOCK - 1), last_one, 0.0)
            cum_across = cum_across + jnp.where(
                place == head, jnp.sum(spread_grad, axis=0, keepdims=True), 0.0
            )
            beta_grad = beta_grad + jnp.where(lane == heads + head, beta_one, 0.0)
            score_grad = score_grad * within
            gram_grad = jnp.where(strict, lower_grad * within, 0.0) * beta
            by_key = mm_back(jnp.concatenate([score_grad, gram_grad], axis=0), key)
            query_grad = initial * query_grad + by_key[:BLOCK]
            key_grad = (
                (beta * initial) * written_grad
                + tail * tail_grad
                + by_key[BLOCK:]
                + mm_back(gram_grad, key, TN)
                + mm_back(score_grad, query, TN)
            )
            key_grad = key_scale * (
                key_grad - key * jnp.sum(key_grad * key, axis=-1, keepdims=True)
            )
            act_grad_ref[rows, key_cols] = query_grad * query_slope
            act_grad_ref[rows, key_act] = key_grad * key_slope
            act_grad_ref[rows, value_act] = (beta * scaled_grad) * value_slope
        cum_grad = cum_grad - cum_across.T
        rate_grad = mm_sum(lower_ones(), cum_grad, TN)
        logit_grad = rate_grad * (-jnp.exp(decay_ref[0:1, :])) * sigmoid(logits)
        decay_grad_ref[0:1, :] += jnp.sum(rate_grad * rate, axis=0, keepdims=True)
        decay_grad_ref[1:2, :] += jnp.sum(logit_grad, axis=0, keepdims=True)
        out_ref[rows, tail_at : tail_at + TAIL] = jnp.where(
            lane < heads, logit_grad, beta_grad * beta_tile * (1.0 - beta_tile)
        ).astype(out_ref.dtype)
        return 0

    third(pl.program_id(0), 0)

    def fourth(block, _):
        start = pl.multiple_of(block * BLOCK, BLOCK)
        rows = pl.ds(start, BLOCK)
        positions = start + lax.broadcasted_iota(jnp.int32, (BLOCK + 8, 1), 0)
        since = positions - document_starts(lengths_ref, positions)
        for low, high in (
            (0, key_dim),
            (key_dim, 2 * key_dim),
            (2 * key_dim, 2 * key_dim + value_dim),
        ):
            columns = slice(low, high)
            later = jnp.concatenate(
                [
                    act_grad_ref[rows, columns],
                    act_grad_ref[pl.ds(pl.multiple_of(start + BLOCK, 8), 8), columns],
                ],
                axis=0,
            )
            seen = window_before(proj_ref, start, columns)
            here = later[:BLOCK]
            summed = here * filter_ref[CONV - 1 : CONV, columns]
            filter_grad_ref[CONV - 1 : CONV, columns] += jnp.sum(
                here * seen[8:], axis=0, keepdims=True
            )
            for offset in range(1, CONV):
                tap = CONV - 1 - offset
                mask = (since >= offset).astype(jnp.float32)
                summed = summed + later[offset : offset + BLOCK] * (
                    mask[offset : offset + BLOCK] * filter_ref[tap : tap + 1, columns]
                )
                filter_grad_ref[tap : tap + 1, columns] += jnp.sum(
                    here * (mask[:BLOCK] * seen[8 - offset : 8 - offset + BLOCK]),
                    axis=0,
                    keepdims=True,
                )
            out_ref[rows, columns] = summed.astype(out_ref.dtype)
        return 0

    @pl.when(pl.program_id(0) == blocks - 1)
    def _():
        lax.fori_loop(0, blocks, fourth, 0, unroll=4)


def f32(*shape):
    return jax.ShapeDtypeStruct(shape, jnp.float32)


VMEM = pl.BlockSpec(memory_space=pltpu.VMEM)
SMEM = pl.BlockSpec(memory_space=pltpu.SMEM)
PARAMS = pltpu.CompilerParams(vmem_limit_bytes=60 * 2**20)


def mixer_forward(lengths, proj, gate, filters, decay_pair, out_gain, heads):
    length = proj.shape[0]
    pairs = length // BLOCK * heads * BLOCK
    key_dim, value_dim = heads * KH, heads * VH
    return pl.pallas_call(
        functools.partial(forward_kernel, heads),
        out_shape=(
            jax.ShapeDtypeStruct((length, value_dim), jnp.bfloat16),
            f32(length, 2 * key_dim + value_dim),
            f32(pairs, BLOCK),
            f32(pairs, VH),
            f32(length, value_dim),
            f32(length, value_dim),
            f32(pairs, BLOCK),
            f32(pairs, BLOCK),
            f32(length, key_dim),
            f32(pairs, KH),
        ),
        in_specs=[SMEM] + [VMEM] * 5,
        out_specs=(VMEM,) * 10,
        scratch_shapes=[
            pltpu.VMEM((length, value_dim), jnp.float32),
            pltpu.VMEM((length, key_dim), jnp.float32),
            pltpu.VMEM((pairs, VH), jnp.float32),
        ],
        compiler_params=PARAMS,
        cost_estimate=pl.CostEstimate(
            flops=20 * 10**9, bytes_accessed=2**20, transcendentals=0
        ),
        name="mixer_forward",
    )(lengths, proj, gate, filters, decay_pair, out_gain)


def gate_backward(grad, gate, out_gain, result, query, step, heads):
    length = gate.shape[0]
    pairs = length // BLOCK * heads * BLOCK
    value_dim = heads * VH
    return pl.pallas_call(
        functools.partial(gate_back_kernel, heads),
        out_shape=(
            jax.ShapeDtypeStruct(gate.shape, jnp.bfloat16),
            f32(8, VH),
            f32(length, value_dim),
            f32(pairs, VH),
        ),
        in_specs=[VMEM] * 6,
        out_specs=(VMEM,) * 4,
        compiler_params=PARAMS,
        cost_estimate=pl.CostEstimate(flops=10**6, bytes_accessed=2**10, transcendentals=0),
        name="gate_backward",
    )(grad, gate, out_gain, result, query, step)


def whole(item):
    return pl.BlockSpec(item.shape, lambda block: (0, 0), pipeline_mode=pl.Buffered(1))


def turn(item, length):
    return pl.BlockSpec((item.shape[0] * BLOCK // length, item.shape[1]), lambda block: (block, 0))


def rule_backward(lengths, proj, filters, decay_pair, kept, back, reach, heads):
    length = proj.shape[0]
    conv_dim = filters.shape[1]
    return pl.pallas_call(
        functools.partial(rule_back_kernel, heads),
        out_shape=(
            jax.ShapeDtypeStruct(proj.shape, jnp.bfloat16),
            f32(CONV, conv_dim),
            f32(8, TAIL),
        ),
        grid=(length // BLOCK,),
        in_specs=[SMEM, whole(proj), whole(filters), whole(decay_pair)]
        + [turn(item, length) for item in (*kept, back, reach)],
        out_specs=(
            pl.BlockSpec(proj.shape, lambda block: (0, 0)),
            pl.BlockSpec((CONV, conv_dim), lambda block: (0, 0)),
            pl.BlockSpec((8, TAIL), lambda block: (0, 0)),
        ),
        scratch_shapes=[pltpu.VMEM((length + 8, conv_dim), jnp.float32)],
        compiler_params=PARAMS,
        cost_estimate=pl.CostEstimate(flops=10**6, bytes_accessed=2**10, transcendentals=0),
        name="rule_backward",
    )(lengths, proj, filters, decay_pair, *kept, back, reach)


def plain_product(first_mat, second_mat):
    return jnp.dot(first_mat, second_mat, preferred_element_type=jnp.float32)


def left_product(first_mat, second_mat):
    return lax.dot_general(first_mat, second_mat, TN, preferred_element_type=jnp.float32)


def right_product(first_mat, second_mat):
    return lax.dot_general(first_mat, second_mat, NT, preferred_element_type=jnp.float32)


def rms_scale(values, scales):
    return values * lax.rsqrt(jnp.mean(values * values, axis=-1, keepdims=True) + epsilon) * scales


def norm_back(inputs, scales, grad_normed):
    inverse = lax.rsqrt(jnp.mean(inputs * inputs, axis=-1, keepdims=True) + epsilon)
    weighted = scales * grad_normed
    grad_inputs = inverse * weighted - inputs * (inverse * inverse * inverse) * jnp.mean(
        weighted * inputs, axis=-1, keepdims=True
    )
    grad_scales = jnp.sum(grad_normed * inputs * inverse, axis=0)
    return (grad_inputs, grad_scales)


def swap(values, axis):
    return lax.ppermute(values, axis, [(0, 1), (1, 0)])


def joined(own, other, axis):
    leads = lax.axis_index(axis) == 0
    return jnp.concatenate(
        [jnp.where(leads, own, other), jnp.where(leads, other, own)], axis=1
    )


def gather_features(own):
    half = joined(own, swap(own, "col"), "col")
    return joined(half, swap(half, "row"), "row")


def half_of(values, index):
    width = values.shape[1] // 2
    return lax.dynamic_slice_in_dim(values, index * width, width, 1)


def scatter_step(partial, axis):
    index = lax.axis_index(axis)
    other = swap(half_of(partial, 1 - index).astype(jnp.bfloat16), axis)
    return half_of(partial, index) + other.astype(jnp.float32)


def pair_total(partial, axis):
    low = partial.astype(jnp.bfloat16)
    return low.astype(jnp.float32) + swap(low, axis).astype(jnp.float32)


def scatter_features(partial):
    return scatter_step(scatter_step(partial, "row"), "col")


def bit_swap(values, axis, bit):
    count = lax.axis_size(axis)
    return lax.ppermute(values, axis, [(place, place ^ (1 << bit)) for place in range(count)])


def small_total(values, axis):
    return values + swap(values, axis)


def small_step(values, axis, bit):
    return values + bit_swap(values, axis, bit) if lax.axis_size(axis) == 8 else values


def totals_step(part, axis, order, step):
    place = lax.axis_index(axis)
    bit = order[min(step, 4 - step)]
    if step < 2:
        mine = (place >> bit) & 1
        half = part.shape[0] // 2
        other = lax.dynamic_slice_in_dim(part, (1 - mine) * half, half, 0)
        got = bit_swap(other.astype(jnp.bfloat16), axis, bit)
        part = lax.dynamic_slice_in_dim(part, mine * half, half, 0) + got.astype(jnp.float32)
        return part.astype(jnp.bfloat16) if step == 1 else part
    got = bit_swap(part, axis, bit)
    if step == 2:
        return (part.astype(jnp.float32) + got.astype(jnp.float32)).astype(jnp.bfloat16)
    leads = ((place >> bit) & 1) == 0
    part = jnp.concatenate([jnp.where(leads, part, got), jnp.where(leads, got, part)], axis=0)
    return part.astype(jnp.float32) if step == 4 else part


def body(
    tokens,
    cotangent,
    lengths,
    norm_gain,
    w_query,
    w_key,
    w_value,
    w_alpha,
    w_beta,
    conv_query,
    conv_key,
    conv_value,
    decay_log,
    decay_bias,
    w_outgate,
    out_gain,
    w_out,
    ffn_gain,
    w_gate,
    w_up,
    w_down,
):
    heads = w_alpha.shape[1]
    key_dim, value_dim = heads * KH, heads * VH
    small = jnp.zeros((w_alpha.shape[0], TAIL - 2 * heads), w_alpha.dtype)
    weights = jnp.concatenate([w_query, w_key, w_value, w_alpha, w_beta, small], axis=1)
    filters = jnp.concatenate([conv_query, conv_key, conv_value], axis=1)
    decay_pair = jnp.pad(jnp.stack([decay_log, decay_bias]), ((0, 6), (0, TAIL - heads)))
    gain_row = out_gain[None]

    tokens_other, weights = lax.optimization_barrier((swap(tokens, "col"), weights))
    tokens_half = joined(tokens, tokens_other, "col")
    whole = joined(tokens_half, swap(tokens_half, "row"), "row").astype(jnp.float32)
    normed = rms_scale(whole, norm_gain).astype(jnp.bfloat16)
    proj = plain_product(normed, weights)
    gate = plain_product(normed, w_outgate)
    later, gate = lax.optimization_barrier((cotangent, gate))
    grad_out_half = joined(later, swap(later, "col"), "col")
    mixed, act, inverse, state, delta, result, score, gram, query, step = mixer_forward(
        lengths, proj, gate, filters, decay_pair, gain_row, heads
    )
    mixed, grad_out_half = lax.optimization_barrier((mixed, grad_out_half))
    hidden_half = tokens_half.astype(jnp.float32) + pair_total(
        scatter_step(plain_product(mixed, w_out), "row"), "col"
    )
    hidden_own = half_of(hidden_half, lax.axis_index("col"))
    hidden_low = hidden_half.astype(jnp.bfloat16)
    hidden = joined(hidden_low, swap(hidden_low, "row"), "row").astype(jnp.float32)
    normed_ffn = rms_scale(hidden, ffn_gain).astype(jnp.bfloat16)
    gate_act = plain_product(normed_ffn, w_gate)
    up_act = plain_product(normed_ffn, w_up)
    sigma = jax.nn.sigmoid(gate_act)
    product = (gate_act * sigma * up_act).astype(jnp.bfloat16)
    grad_out = joined(grad_out_half, swap(grad_out_half, "row"), "row")
    grad_product = right_product(grad_out, w_down)
    grad_gate_act = (grad_product * up_act * sigma * (1.0 + gate_act * (1.0 - sigma))).astype(
        jnp.bfloat16
    )
    grad_up_act = (grad_product * gate_act * sigma).astype(jnp.bfloat16)
    grad_normed_ffn = right_product(grad_gate_act, w_gate) + right_product(grad_up_act, w_up)
    grad_hidden_part, grad_ffn_gain = norm_back(hidden, ffn_gain, grad_normed_ffn)
    grad_down = left_product(product, grad_out)
    grad_gate = left_product(normed_ffn, grad_gate_act)
    grad_up = left_product(normed_ffn, grad_up_act)
    ffn_grads = tuple(item.astype(jnp.bfloat16) for item in (grad_down, grad_gate, grad_up))
    grad_hidden_half = (
        grad_out_half.astype(jnp.float32)
        + pair_total(scatter_step(grad_hidden_part, "row"), "col")
    ).astype(jnp.bfloat16)
    grad_hidden_half, *ffn_grads = lax.optimization_barrier((grad_hidden_half, *ffn_grads))
    ffn_sums = lax.psum(tuple(ffn_grads), "dp")
    grad_hidden = joined(grad_hidden_half, swap(grad_hidden_half, "row"), "row")
    grad_hidden_own = half_of(grad_hidden_half, lax.axis_index("col"))
    grad_hidden, product_later = lax.optimization_barrier((grad_hidden, product))
    output = (hidden_own + scatter_features(plain_product(product_later, w_down))).astype(jnp.bfloat16)
    grad_mixed = right_product(grad_hidden, w_out)
    order = (0, 1, 2)
    staged = lax.axis_size("dp") == 8

    def advance(part, step):
        return totals_step(part, "dp", order, step) if staged else part

    grad_gate_proj, gain_grad, back, reach = gate_backward(
        grad_mixed, gate, gain_row, result, query, step, heads
    )
    out_part = left_product(grad_hidden, mixed)
    gate_part = left_product(normed, grad_gate_proj)
    out_part, gate_part, back = lax.optimization_barrier((out_part, gate_part, back))
    early = jnp.concatenate([advance(out_part, 0), advance(gate_part, 0)], axis=1)
    grad_proj, filter_grad, decay_grad = rule_backward(
        lengths, proj, filters, decay_pair, (act, inverse, state, delta, score, gram), back, reach, heads
    )
    conv_dim = 2 * key_dim + value_dim
    early, grad_proj = lax.optimization_barrier((early, grad_proj))
    late = left_product(normed, grad_proj[:, :conv_dim])
    early, late = lax.optimization_barrier((early, late))
    early, late = advance(early, 1), advance(late, 0)
    early, late, grad_proj = lax.optimization_barrier((early, late, grad_proj))

    early, late = advance(early, 2), advance(late, 1)
    grad_pair = left_product(normed, grad_proj[:, conv_dim:])
    grad_normed = right_product(grad_proj, weights) + right_product(grad_gate_proj, w_outgate)
    grad_input_part, grad_norm_gain = norm_back(whole, norm_gain, grad_normed)
    grad_input_part = grad_input_part.astype(jnp.bfloat16)
    early, late, grad_input_part, grad_norm_gain, grad_pair = lax.optimization_barrier(
        (early, late, grad_input_part, grad_norm_gain, grad_pair)
    )

    early, late = advance(early, 3), advance(late, 2)
    gains = jnp.concatenate([grad_norm_gain, grad_ffn_gain, gain_grad[0]])
    gains = small_total(small_total(gains, "row"), "col")
    sizes = (
        gains,
        filter_grad.reshape(-1),
        grad_pair[:, : 2 * heads].reshape(-1),
        decay_grad[:2, :heads].reshape(-1),
    )
    small_sum = small_step(jnp.concatenate(sizes), "dp", 0)
    input_row = scatter_step(grad_input_part.astype(jnp.float32), "row")
    early, late, small_sum, input_row, *ffn_sums = lax.optimization_barrier(
        (early, late, small_sum, input_row, *ffn_sums)
    )
    down_sum, gate_sum, up_sum = (item.astype(jnp.float32) for item in ffn_sums)

    early, late = advance(early, 4), advance(late, 3)
    small_sum = small_step(small_sum, "dp", 1)
    input_grad = (
        grad_hidden_own.astype(jnp.float32) + scatter_step(input_row, "col")
    ).astype(jnp.bfloat16)
    early, late, small_sum, input_grad, down_sum, gate_sum, up_sum = lax.optimization_barrier(
        (early, late, small_sum, input_grad, down_sum, gate_sum, up_sum)
    )

    late = advance(late, 4)
    small_sum = small_step(small_sum, "dp", 2)
    if not staged:
        small_sum = lax.psum(small_sum, "dp")
        early, late = (
            item.astype(jnp.float32)
            for item in lax.psum((early.astype(jnp.bfloat16), late.astype(jnp.bfloat16)), "dp")
        )
    out_sum = early[:, :value_dim].T
    gate_weight_sum = early[:, value_dim:]
    query_sum, key_sum = late[:, :key_dim], late[:, key_dim : 2 * key_dim]
    value_sum = late[:, 2 * key_dim :]
    width = norm_gain.shape[0]
    places = [0]
    for item in sizes:
        places.append(places[-1] + item.shape[0])
    pieces = [small_sum[low:high] for low, high in zip(places, places[1:])]
    filter_sum = pieces[1].reshape(filters.shape)
    pair_sum = pieces[2].reshape(-1, 2 * heads)
    decay_sum = pieces[3].reshape(2, heads)
    return (
        output,
        input_grad,
        pieces[0][:width],
        query_sum,
        key_sum,
        value_sum,
        pair_sum[:, :heads],
        pair_sum[:, heads:],
        filter_sum[:, :key_dim],
        filter_sum[:, key_dim : 2 * key_dim],
        filter_sum[:, 2 * key_dim :],
        decay_sum[0],
        decay_sum[1],
        gate_weight_sum,
        pieces[0][2 * width :],
        out_sum,
        pieces[0][width : 2 * width],
        gate_sum,
        up_sum,
        down_sum,
    )


def solution(mesh):
    placed = (
        P("dp", ("row", "col")),
        P("dp", ("row", "col")),
        P("dp", None),
        P(),
        P(None, ("row", "col")),
        P(None, ("row", "col")),
        P(None, ("row", "col")),
        P(None, ("row", "col")),
        P(None, ("row", "col")),
        P(None, ("row", "col")),
        P(None, ("row", "col")),
        P(None, ("row", "col")),
        P(("row", "col")),
        P(("row", "col")),
        P(None, ("row", "col")),
        P(),
        P(("row", "col"), None),
        P(),
        P(None, ("row", "col")),
        P(None, ("row", "col")),
        P(("row", "col"), None),
    )
    return jax.shard_map(
        body,
        mesh=mesh,
        in_specs=placed,
        out_specs=(
            P("dp", ("row", "col")),
            P("dp", ("row", "col")),
            P(),
            P(None, ("row", "col")),
            P(None, ("row", "col")),
            P(None, ("row", "col")),
            P(None, ("row", "col")),
            P(None, ("row", "col")),
            P(None, ("row", "col")),
            P(None, ("row", "col")),
            P(None, ("row", "col")),
            P(("row", "col")),
            P(("row", "col")),
            P(None, ("row", "col")),
            P(),
            P(("row", "col"), None),
            P(),
            P(None, ("row", "col")),
            P(None, ("row", "col")),
            P(("row", "col"), None),
        ),
        check_vma=False,
    )
```

```python
import functools

import jax
import jax.numpy as jnp
from jax import lax
from jax.experimental import pallas as pl
from jax.experimental.pallas import tpu as pltpu
from jax.sharding import PartitionSpec as P

KH = 128
VH = 256
CONV = 4
BLOCK = 128
TAIL = 128
GROUP = 4

epsilon = 1e-06
out_epsilon = 0.05

NN = (((1,), (0,)), ((), ()))
NT = (((1,), (1,)), ((), ()))
TN = (((0,), (0,)), ((), ()))


def product_one(first, second, dims=NN):
    return lax.dot_general(
        first.astype(jnp.bfloat16),
        second.astype(jnp.bfloat16),
        dims,
        preferred_element_type=jnp.float32,
    )


def product_three(first, second, dims=NN):
    (along_first,), (along_second,) = dims[0]
    across = 1 - along_second
    first_high = first.astype(jnp.bfloat16)
    second_high = second.astype(jnp.bfloat16)
    first_low = (first - first_high.astype(jnp.float32)).astype(jnp.bfloat16)
    second_low = (second - second_high.astype(jnp.float32)).astype(jnp.bfloat16)
    dot = functools.partial(
        lax.dot_general, dimension_numbers=dims, preferred_element_type=jnp.float32
    )
    short = first.shape[along_first] <= 128
    narrow = second.shape[across] <= 128
    count = second.shape[across]
    if short:
        stacked = jnp.concatenate([first_high, first_low], axis=along_first)
    if short and narrow:
        over = jnp.concatenate([second_high, second_low], axis=across)
        under = jnp.concatenate([second_high, jnp.zeros_like(second_low)], axis=across)
        both = dot(stacked, jnp.concatenate([over, under], axis=along_second))
        return both[:, :count] + both[:, count:]
    if short:
        twice = jnp.concatenate([second_high, second_high], axis=along_second)
        return dot(stacked, twice) + dot(first_high, second_low)
    if narrow:
        both = dot(first_high, jnp.concatenate([second_high, second_low], axis=across))
        return both[:, :count] + (both[:, count:] + dot(first_low, second_high))
    return dot(first_high, second_high) + (
        dot(first_high, second_low) + dot(first_low, second_high)
    )


def product_six(first, second, dims=NN):
    return lax.dot_general(
        first, second, dims, precision=lax.Precision.HIGHEST, preferred_element_type=jnp.float32
    )


mm_sum = product_six
mm_inverse = product_three
mm_chain = product_three
mm_gram = product_three
mm_out = product_three
mm_back = product_three


def sigmoid(values):
    return 1.0 / (1.0 + jnp.exp(-values))


def softplus(values):
    return jnp.maximum(values, 0.0) + jnp.log1p(jnp.exp(-jnp.abs(values)))


def document_starts(lengths_ref, positions):
    starts = jnp.zeros_like(positions)
    end = 0
    for doc in range(lengths_ref.shape[1] - 1):
        end = end + lengths_ref[0, doc]
        starts = jnp.where(positions >= end, end, starts)
    return starts


def start_of(lengths_ref, position):
    start = 0
    end = 0
    for doc in range(lengths_ref.shape[1] - 1):
        end = end + lengths_ref[0, doc]
        start = jnp.where(position >= end, end, start)
    return start


def unit_inverses(lowers):
    size = lowers[0].shape[0]
    row = lax.broadcasted_iota(jnp.int32, (size, size), 0)
    column = lax.broadcasted_iota(jnp.int32, (size, size), 1)
    eye = (row == column).astype(jnp.float32)
    within = (row >> 3) == (column >> 3)
    inner = [jnp.where(within, low, 0.0) for low in lowers]
    square = [mm_inverse(one, one) for one in inner]
    cube = [mm_inverse(one, two) for one, two in zip(inner, square)]
    fourth = [mm_inverse(two, two) for two in square]
    part = [eye - one + two - three for one, two, three in zip(inner, square, cube)]
    result = [one + mm_inverse(one, four) for one, four in zip(part, fourth)]
    shift = 3
    while (1 << shift) < size:
        off = ((row >> (shift + 1)) == (column >> (shift + 1))) & (
            (row >> shift) != (column >> shift)
        )
        edge = [mm_inverse(jnp.where(off, low, 0.0), one) for low, one in zip(lowers, result)]
        result = [one - mm_inverse(one, two) for one, two in zip(result, edge)]
        shift += 1
    return result


def window_before(ref, start, columns):
    early = pl.multiple_of(jnp.maximum(start - 8, 0), 8)
    return jnp.concatenate(
        [ref[pl.ds(early, 8), columns], ref[pl.ds(start, BLOCK), columns]], axis=0
    )


def decays(tail, scales, biases):
    logits = tail + biases
    return -jnp.exp(scales) * softplus(logits), logits


def block_masks(lengths_ref, start):
    positions = start + lax.broadcasted_iota(jnp.int32, (BLOCK, 1), 0)
    starts = document_starts(lengths_ref, positions)
    columns = start + lax.broadcasted_iota(jnp.int32, (BLOCK, BLOCK), 1)
    rows = start + lax.broadcasted_iota(jnp.int32, (BLOCK, BLOCK), 0)
    linked = (starts <= columns) & (rows >= columns)
    strict = rows > columns
    carried = (starts < start).astype(jnp.float32)
    last_start = start_of(lengths_ref, start + BLOCK - 1)
    tail_mask = (positions >= last_start).astype(jnp.float32)
    last_carried = (last_start < start).astype(jnp.float32)
    return positions - starts, linked, strict, carried, tail_mask, last_carried


def lower_ones():
    row = lax.broadcasted_iota(jnp.int32, (BLOCK, BLOCK), 0)
    column = lax.broadcasted_iota(jnp.int32, (BLOCK, BLOCK), 1)
    return (row >= column).astype(jnp.float32)


def head_decay(cumulative, flipped, head, linked, carried, tail_mask, last_carried):
    cum = cumulative[:, head : head + 1]
    spread = cum - flipped[head : head + 1, :]
    within = jnp.where(linked, jnp.exp(jnp.where(linked, spread, 0.0)), 0.0)
    last = cumulative[BLOCK - 1 : BLOCK, head : head + 1]
    initial = jnp.exp(cum) * carried
    tail = jnp.exp(last - cum) * tail_mask
    end = jnp.exp(last) * last_carried
    return within, initial, tail, end


def forward_kernel(
    heads,
    lengths_ref,
    proj_ref,
    gate_ref,
    filter_ref,
    decay_ref,
    gain_ref,
    mixed_ref,
    act_ref,
    inverse_ref,
    state_ref,
    delta_ref,
    result_ref,
    score_ref,
    gram_ref,
    query_ref,
    step_ref,
    pseudo_ref,
    correct_ref,
    add_ref,
):
    length = proj_ref.shape[0]
    blocks = length // BLOCK
    key_dim, value_dim = heads * KH, heads * VH
    tail_at = 2 * key_dim + value_dim
    widths = ((0, key_dim), (key_dim, 2 * key_dim), (2 * key_dim, 2 * key_dim + value_dim))

    def first(turn, _):
        lowers, kept = [], []
        for lane in range(GROUP):
            block = turn * GROUP + lane
            start = pl.multiple_of(block * BLOCK, BLOCK)
            rows = pl.ds(start, BLOCK)
            since, linked, strict, carried, tail_mask, last_carried = block_masks(
                lengths_ref, start
            )
            parts = []
            for low, high in widths:
                columns = slice(low, high)
                seen = window_before(proj_ref, start, columns)
                summed = seen[8:] * filter_ref[CONV - 1 : CONV, columns]
                for offset in range(1, CONV):
                    tap = CONV - 1 - offset
                    mask = (since >= offset).astype(jnp.float32)
                    summed = summed + seen[8 - offset : 8 - offset + BLOCK] * (
                        mask * filter_ref[tap : tap + 1, columns]
                    )
                act_ref[rows, columns] = summed
                parts.append(summed * sigmoid(summed))
            tail_tile = proj_ref[rows, tail_at : tail_at + TAIL]
            rate, _ = decays(tail_tile, decay_ref[0:1, :], decay_ref[1:2, :])
            beta_tile = sigmoid(tail_tile)
            cumulative = mm_sum(lower_ones(), rate)
            flipped = cumulative.T
            for head in range(heads):
                within, initial, tail, end = head_decay(
                    cumulative, flipped, head, linked, carried, tail_mask, last_carried
                )
                beta = beta_tile[:, heads + head : heads + head + 1]
                query = parts[0][:, head * KH : (head + 1) * KH]
                key = parts[1][:, head * KH : (head + 1) * KH]
                key = key * lax.rsqrt(jnp.sum(key * key, axis=-1, keepdims=True) + epsilon)
                value = parts[2][:, head * VH : (head + 1) * VH]
                both = mm_gram(jnp.concatenate([key, query], axis=0), key, NT)
                gram = both[:BLOCK] * jnp.where(strict, within, 0.0)
                score = both[BLOCK:] * within
                lowers.append(beta * gram)
                at = pl.ds(pl.multiple_of((block * heads + head) * BLOCK, BLOCK), BLOCK)
                gram_ref[at, :] = gram
                score_ref[at, :] = score
                query_ref[rows, head * KH : (head + 1) * KH] = query * initial
                kept.append((rows, at, head, key, value, beta, initial, tail, end))
        inverses = unit_inverses(lowers)
        row = lax.broadcasted_iota(jnp.int32, (KH, KH), 0)
        column = lax.broadcasted_iota(jnp.int32, (KH, KH), 1)
        solved = []
        for inverse, (rows, at, head, key, value, beta, initial, tail, end) in zip(inverses, kept):
            inverse_ref[at, :] = inverse
            pseudo = mm_out(inverse, beta * value)
            correct = mm_out(inverse, (beta * initial) * key)
            solved.append((pseudo, correct))
        for (pseudo, correct), (rows, at, head, key, value, beta, initial, tail, end) in zip(
            solved, kept
        ):
            tail_key = tail * key
            step = jnp.where(row == column, end, 0.0) - mm_chain(tail_key, correct, TN)
            pseudo_ref[rows, head * VH : (head + 1) * VH] = pseudo
            correct_ref[rows, head * KH : (head + 1) * KH] = correct
            step_ref[at, :] = step
            add_ref[at, :] = mm_chain(tail_key, pseudo, TN)
        return 0

    lax.fori_loop(0, blocks // GROUP, first, 0)

    def second(block, states):
        after = []
        for head in range(heads):
            at = pl.ds(pl.multiple_of((block * heads + head) * BLOCK, BLOCK), BLOCK)
            state_ref[at, :] = states[head]
            after.append(mm_chain(step_ref[at, :], states[head]) + add_ref[at, :])
        return tuple(after)

    lax.fori_loop(
        0, blocks, second, tuple(jnp.zeros((KH, VH), jnp.float32) for _ in range(heads))
    )

    def third(block, _):
        start = pl.multiple_of(block * BLOCK, BLOCK)
        rows = pl.ds(start, BLOCK)
        for head in range(heads):
            at = pl.ds(pl.multiple_of((block * heads + head) * BLOCK, BLOCK), BLOCK)
            key_cols = slice(head * KH, (head + 1) * KH)
            value_cols = slice(head * VH, (head + 1) * VH)
            state = state_ref[at, :]
            score = score_ref[at, :]
            correct = correct_ref[rows, key_cols]
            query = query_ref[rows, key_cols]
            delta = pseudo_ref[rows, value_cols] - mm_out(correct, state)
            result = mm_out(query, state) + mm_out(score, delta)
            delta_ref[rows, value_cols] = delta
            result_ref[rows, value_cols] = result
            query_ref[rows, key_cols] = query - mm_out(score, correct)
            gate = gate_ref[rows, value_cols]
            scale = lax.rsqrt(jnp.mean(result * result, axis=-1, keepdims=True) + out_epsilon)
            mixed = result * scale * gain_ref[...] * (gate * sigmoid(gate))
            mixed_ref[rows, value_cols] = mixed.astype(mixed_ref.dtype)
        return 0

    lax.fori_loop(0, blocks, third, 0, unroll=4)


def gate_back_kernel(
    heads,
    grad_ref,
    gate_ref,
    gain_ref,
    result_ref,
    query_ref,
    step_ref,
    out_ref,
    gain_grad_ref,
    back_ref,
    reach_ref,
):
    length = gate_ref.shape[0]
    blocks = length // BLOCK
    gain_grad_ref[...] = jnp.zeros_like(gain_grad_ref)

    def first(block, _):
        start = pl.multiple_of(block * BLOCK, BLOCK)
        rows = pl.ds(start, BLOCK)
        for head in range(heads):
            at = pl.ds(pl.multiple_of((block * heads + head) * BLOCK, BLOCK), BLOCK)
            key_cols = slice(head * KH, (head + 1) * KH)
            value_cols = slice(head * VH, (head + 1) * VH)
            result = result_ref[rows, value_cols]
            gate = gate_ref[rows, value_cols]
            grad = grad_ref[rows, value_cols]
            sigma = sigmoid(gate)
            scale = lax.rsqrt(jnp.mean(result * result, axis=-1, keepdims=True) + out_epsilon)
            normed = result * scale
            out_ref[rows, value_cols] = (
                grad * normed * gain_ref[...] * (sigma * (1.0 + gate * (1.0 - sigma)))
            ).astype(out_ref.dtype)
            grad = grad * (gate * sigma)
            gain_grad_ref[0:1, :] += jnp.sum(grad * normed, axis=0, keepdims=True)
            grad = grad * gain_ref[...]
            grad = scale * (grad - normed * jnp.mean(grad * normed, axis=-1, keepdims=True))
            back_ref[rows, value_cols] = grad
            reach_ref[at, :] = mm_chain(query_ref[rows, key_cols], grad, TN)
        return 0

    lax.fori_loop(0, blocks, first, 0, unroll=4)

    def second(index, states):
        block = blocks - 1 - index
        after = []
        for head in range(heads):
            at = pl.ds(pl.multiple_of((block * heads + head) * BLOCK, BLOCK), BLOCK)
            reach = reach_ref[at, :]
            reach_ref[at, :] = states[head]
            after.append(mm_chain(step_ref[at, :], states[head], TN) + reach)
        return tuple(after)

    lax.fori_loop(
        0, blocks, second, tuple(jnp.zeros((KH, VH), jnp.float32) for _ in range(heads))
    )

def rule_back_kernel(
    heads,
    lengths_ref,
    proj_ref,
    filter_ref,
    decay_ref,
    act_ref,
    inverse_ref,
    state_ref,
    delta_ref,
    score_ref,
    gram_ref,
    back_ref,
    reach_ref,
    out_ref,
    filter_grad_ref,
    decay_grad_ref,
    act_grad_ref,
):
    length = proj_ref.shape[0]
    blocks = length // BLOCK
    key_dim, value_dim = heads * KH, heads * VH
    conv_dim = 2 * key_dim + value_dim
    tail_at = conv_dim

    @pl.when(pl.program_id(0) == 0)
    def _():
        filter_grad_ref[...] = jnp.zeros_like(filter_grad_ref)
        decay_grad_ref[...] = jnp.zeros_like(decay_grad_ref)
        act_grad_ref[length : length + 8, :] = jnp.zeros((8, conv_dim), jnp.float32)

    def third(block, _):
        start = pl.multiple_of(block * BLOCK, BLOCK)
        rows = pl.ds(start, BLOCK)
        since, linked, strict, carried, tail_mask, last_carried = block_masks(lengths_ref, start)
        tail_tile = proj_ref[rows, tail_at : tail_at + TAIL]
        rate, logits = decays(tail_tile, decay_ref[0:1, :], decay_ref[1:2, :])
        beta_tile = sigmoid(tail_tile)
        cumulative = mm_sum(lower_ones(), rate)
        flipped = cumulative.T
        lane = lax.broadcasted_iota(jnp.int32, (BLOCK, TAIL), 1)
        place = lax.broadcasted_iota(jnp.int32, (BLOCK, TAIL), 0)
        cum_grad = jnp.zeros((BLOCK, TAIL), jnp.float32)
        cum_across = jnp.zeros((TAIL, BLOCK), jnp.float32)
        beta_grad = jnp.zeros((BLOCK, TAIL), jnp.float32)
        for head in range(heads):
            at = slice(head * BLOCK, (head + 1) * BLOCK)
            key_cols = slice(head * KH, (head + 1) * KH)
            key_act = slice(key_dim + head * KH, key_dim + (head + 1) * KH)
            value_act = slice(2 * key_dim + head * VH, 2 * key_dim + (head + 1) * VH)
            value_cols = slice(head * VH, (head + 1) * VH)
            within, initial, tail, end = head_decay(
                cumulative, flipped, head, linked, carried, tail_mask, last_carried
            )
            beta = beta_tile[:, heads + head : heads + head + 1]
            summed = act_ref[:, key_cols]
            query_sigma = sigmoid(summed)
            query = summed * query_sigma
            query_slope = query_sigma * (1.0 + summed * (1.0 - query_sigma))
            summed = act_ref[:, key_act]
            key_sigma = sigmoid(summed)
            key = summed * key_sigma
            key_slope = key_sigma * (1.0 + summed * (1.0 - key_sigma))
            key_scale = lax.rsqrt(jnp.sum(key * key, axis=-1, keepdims=True) + epsilon)
            key = key * key_scale
            summed = act_ref[:, value_act]
            value_sigma = sigmoid(summed)
            value = summed * value_sigma
            value_slope = value_sigma * (1.0 + summed * (1.0 - value_sigma))
            grad = back_ref[:, value_cols]
            after = reach_ref[at, :]
            state = state_ref[at, :]
            score = score_ref[at, :]
            gram = gram_ref[at, :]
            delta = delta_ref[:, value_cols]
            tail_key = tail * key
            delta_grad = mm_back(score, grad, TN) + mm_back(tail_key, after)
            scaled_grad = mm_back(inverse_ref[at, :], delta_grad, TN)
            pair = jnp.concatenate([grad, scaled_grad], axis=0)
            by_state = mm_back(pair, state, NT)
            query_grad = by_state[:BLOCK]
            written_grad = -by_state[BLOCK:]
            by_delta = mm_back(pair, delta, NT)
            tail_grad = mm_back(delta, after, NT)
            score_grad = by_delta[:BLOCK]
            lower_grad = -by_delta[BLOCK:]
            initial_key = initial * key
            beta_one = (
                jnp.sum(scaled_grad * value, axis=-1, keepdims=True)
                + jnp.sum(written_grad * initial_key, axis=-1, keepdims=True)
                + jnp.sum(lower_grad * gram, axis=-1, keepdims=True)
            )
            spread_grad = score_grad * score + lower_grad * (beta * gram)
            tail_one = tail * jnp.sum(tail_grad * key, axis=-1, keepdims=True)
            initial_one = initial * (
                jnp.sum(query_grad * query, axis=-1, keepdims=True)
                + beta * jnp.sum(written_grad * key, axis=-1, keepdims=True)
            )
            last_one = jnp.sum(tail_one, axis=0, keepdims=True) + end * jnp.sum(
                jnp.sum(state * after, axis=-1, keepdims=True), axis=0, keepdims=True
            )
            cum_one = jnp.sum(spread_grad, axis=-1, keepdims=True) + initial_one - tail_one
            cum_grad = cum_grad + jnp.where(lane == head, cum_one, 0.0)
            cum_grad = cum_grad + jnp.where((lane == head) & (place == BLOCK - 1), last_one, 0.0)
            cum_across = cum_across + jnp.where(
                place == head, jnp.sum(spread_grad, axis=0, keepdims=True), 0.0
            )
            beta_grad = beta_grad + jnp.where(lane == heads + head, beta_one, 0.0)
            score_grad = score_grad * within
            gram_grad = jnp.where(strict, lower_grad * within, 0.0) * beta
            by_key = mm_back(jnp.concatenate([score_grad, gram_grad], axis=0), key)
            query_grad = initial * query_grad + by_key[:BLOCK]
            key_grad = (
                (beta * initial) * written_grad
                + tail * tail_grad
                + by_key[BLOCK:]
                + mm_back(gram_grad, key, TN)
                + mm_back(score_grad, query, TN)
            )
            key_grad = key_scale * (
                key_grad - key * jnp.sum(key_grad * key, axis=-1, keepdims=True)
            )
            act_grad_ref[rows, key_cols] = query_grad * query_slope
            act_grad_ref[rows, key_act] = key_grad * key_slope
            act_grad_ref[rows, value_act] = (beta * scaled_grad) * value_slope
        cum_grad = cum_grad - cum_across.T
        rate_grad = mm_sum(lower_ones(), cum_grad, TN)
        logit_grad = rate_grad * (-jnp.exp(decay_ref[0:1, :])) * sigmoid(logits)
        decay_grad_ref[0:1, :] += jnp.sum(rate_grad * rate, axis=0, keepdims=True)
        decay_grad_ref[1:2, :] += jnp.sum(logit_grad, axis=0, keepdims=True)
        out_ref[rows, tail_at : tail_at + TAIL] = jnp.where(
            lane < heads, logit_grad, beta_grad * beta_tile * (1.0 - beta_tile)
        ).astype(out_ref.dtype)
        return 0

    third(pl.program_id(0), 0)

    def fourth(block, _):
        start = pl.multiple_of(block * BLOCK, BLOCK)
        rows = pl.ds(start, BLOCK)
        positions = start + lax.broadcasted_iota(jnp.int32, (BLOCK + 8, 1), 0)
        since = positions - document_starts(lengths_ref, positions)
        for low, high in (
            (0, key_dim),
            (key_dim, 2 * key_dim),
            (2 * key_dim, 2 * key_dim + value_dim),
        ):
            columns = slice(low, high)
            later = jnp.concatenate(
                [
                    act_grad_ref[rows, columns],
                    act_grad_ref[pl.ds(pl.multiple_of(start + BLOCK, 8), 8), columns],
                ],
                axis=0,
            )
            seen = window_before(proj_ref, start, columns)
            here = later[:BLOCK]
            summed = here * filter_ref[CONV - 1 : CONV, columns]
            filter_grad_ref[CONV - 1 : CONV, columns] += jnp.sum(
                here * seen[8:], axis=0, keepdims=True
            )
            for offset in range(1, CONV):
                tap = CONV - 1 - offset
                mask = (since >= offset).astype(jnp.float32)
                summed = summed + later[offset : offset + BLOCK] * (
                    mask[offset : offset + BLOCK] * filter_ref[tap : tap + 1, columns]
                )
                filter_grad_ref[tap : tap + 1, columns] += jnp.sum(
                    here * (mask[:BLOCK] * seen[8 - offset : 8 - offset + BLOCK]),
                    axis=0,
                    keepdims=True,
                )
            out_ref[rows, columns] = summed.astype(out_ref.dtype)
        return 0

    @pl.when(pl.program_id(0) == blocks - 1)
    def _():
        lax.fori_loop(0, blocks, fourth, 0, unroll=4)


def f32(*shape):
    return jax.ShapeDtypeStruct(shape, jnp.float32)


VMEM = pl.BlockSpec(memory_space=pltpu.VMEM)
SMEM = pl.BlockSpec(memory_space=pltpu.SMEM)
PARAMS = pltpu.CompilerParams(vmem_limit_bytes=60 * 2**20)


def mixer_forward(lengths, proj, gate, filters, decay_pair, out_gain, heads):
    length = proj.shape[0]
    pairs = length // BLOCK * heads * BLOCK
    key_dim, value_dim = heads * KH, heads * VH
    return pl.pallas_call(
        functools.partial(forward_kernel, heads),
        out_shape=(
            jax.ShapeDtypeStruct((length, value_dim), jnp.bfloat16),
            f32(length, 2 * key_dim + value_dim),
            f32(pairs, BLOCK),
            f32(pairs, VH),
            f32(length, value_dim),
            f32(length, value_dim),
            f32(pairs, BLOCK),
            f32(pairs, BLOCK),
            f32(length, key_dim),
            f32(pairs, KH),
        ),
        in_specs=[SMEM] + [VMEM] * 5,
        out_specs=(VMEM,) * 10,
        scratch_shapes=[
            pltpu.VMEM((length, value_dim), jnp.float32),
            pltpu.VMEM((length, key_dim), jnp.float32),
            pltpu.VMEM((pairs, VH), jnp.float32),
        ],
        compiler_params=PARAMS,
        cost_estimate=pl.CostEstimate(
            flops=20 * 10**9, bytes_accessed=2**20, transcendentals=0
        ),
        name="mixer_forward",
    )(lengths, proj, gate, filters, decay_pair, out_gain)


def gate_backward(grad, gate, out_gain, result, query, step, heads):
    length = gate.shape[0]
    pairs = length // BLOCK * heads * BLOCK
    value_dim = heads * VH
    return pl.pallas_call(
        functools.partial(gate_back_kernel, heads),
        out_shape=(
            jax.ShapeDtypeStruct(gate.shape, jnp.bfloat16),
            f32(8, VH),
            f32(length, value_dim),
            f32(pairs, VH),
        ),
        in_specs=[VMEM] * 6,
        out_specs=(VMEM,) * 4,
        compiler_params=PARAMS,
        cost_estimate=pl.CostEstimate(flops=10**6, bytes_accessed=2**10, transcendentals=0),
        name="gate_backward",
    )(grad, gate, out_gain, result, query, step)


def whole(item):
    return pl.BlockSpec(item.shape, lambda block: (0, 0), pipeline_mode=pl.Buffered(1))


def turn(item, length):
    return pl.BlockSpec((item.shape[0] * BLOCK // length, item.shape[1]), lambda block: (block, 0))


def rule_backward(lengths, proj, filters, decay_pair, kept, back, reach, heads):
    length = proj.shape[0]
    conv_dim = filters.shape[1]
    return pl.pallas_call(
        functools.partial(rule_back_kernel, heads),
        out_shape=(
            jax.ShapeDtypeStruct(proj.shape, jnp.bfloat16),
            f32(CONV, conv_dim),
            f32(8, TAIL),
        ),
        grid=(length // BLOCK,),
        in_specs=[SMEM, whole(proj), whole(filters), whole(decay_pair)]
        + [turn(item, length) for item in (*kept, back, reach)],
        out_specs=(
            pl.BlockSpec(proj.shape, lambda block: (0, 0)),
            pl.BlockSpec((CONV, conv_dim), lambda block: (0, 0)),
            pl.BlockSpec((8, TAIL), lambda block: (0, 0)),
        ),
        scratch_shapes=[pltpu.VMEM((length + 8, conv_dim), jnp.float32)],
        compiler_params=PARAMS,
        cost_estimate=pl.CostEstimate(flops=10**6, bytes_accessed=2**10, transcendentals=0),
        name="rule_backward",
    )(lengths, proj, filters, decay_pair, *kept, back, reach)


def plain_product(first_mat, second_mat):
    return jnp.dot(first_mat, second_mat, preferred_element_type=jnp.float32)


def left_product(first_mat, second_mat):
    return lax.dot_general(first_mat, second_mat, TN, preferred_element_type=jnp.float32)


def right_product(first_mat, second_mat):
    return lax.dot_general(first_mat, second_mat, NT, preferred_element_type=jnp.float32)


def rms_scale(values, scales):
    return values * lax.rsqrt(jnp.mean(values * values, axis=-1, keepdims=True) + epsilon) * scales


def norm_back(inputs, scales, grad_normed):
    inverse = lax.rsqrt(jnp.mean(inputs * inputs, axis=-1, keepdims=True) + epsilon)
    weighted = scales * grad_normed
    grad_inputs = inverse * weighted - inputs * (inverse * inverse * inverse) * jnp.mean(
        weighted * inputs, axis=-1, keepdims=True
    )
    grad_scales = jnp.sum(grad_normed * inputs * inverse, axis=0)
    return (grad_inputs, grad_scales)


def swap(values, axis):
    return lax.ppermute(values, axis, [(0, 1), (1, 0)])


def joined(own, other, axis):
    leads = lax.axis_index(axis) == 0
    return jnp.concatenate(
        [jnp.where(leads, own, other), jnp.where(leads, other, own)], axis=1
    )


def gather_features(own):
    half = joined(own, swap(own, "col"), "col")
    return joined(half, swap(half, "row"), "row")


def half_of(values, index):
    width = values.shape[1] // 2
    return lax.dynamic_slice_in_dim(values, index * width, width, 1)


def scatter_step(partial, axis):
    index = lax.axis_index(axis)
    other = swap(half_of(partial, 1 - index).astype(jnp.bfloat16), axis)
    return half_of(partial, index) + other.astype(jnp.float32)


def pair_total(partial, axis):
    low = partial.astype(jnp.bfloat16)
    return low.astype(jnp.float32) + swap(low, axis).astype(jnp.float32)


def scatter_features(partial):
    return scatter_step(scatter_step(partial, "row"), "col")


def bit_swap(values, axis, bit):
    count = lax.axis_size(axis)
    return lax.ppermute(values, axis, [(place, place ^ (1 << bit)) for place in range(count)])


def small_total(values, axis):
    return values + swap(values, axis)


def small_step(values, axis, bit):
    return values + bit_swap(values, axis, bit) if lax.axis_size(axis) == 8 else values


def totals_step(part, axis, order, step):
    place = lax.axis_index(axis)
    bit = order[min(step, 4 - step)]
    if step < 2:
        mine = (place >> bit) & 1
        half = part.shape[0] // 2
        other = lax.dynamic_slice_in_dim(part, (1 - mine) * half, half, 0)
        got = bit_swap(other.astype(jnp.bfloat16), axis, bit)
        part = lax.dynamic_slice_in_dim(part, mine * half, half, 0) + got.astype(jnp.float32)
        return part.astype(jnp.bfloat16) if step == 1 else part
    got = bit_swap(part, axis, bit)
    if step == 2:
        return (part.astype(jnp.float32) + got.astype(jnp.float32)).astype(jnp.bfloat16)
    leads = ((place >> bit) & 1) == 0
    part = jnp.concatenate([jnp.where(leads, part, got), jnp.where(leads, got, part)], axis=0)
    return part.astype(jnp.float32) if step == 4 else part


def body(
    tokens,
    cotangent,
    lengths,
    norm_gain,
    w_query,
    w_key,
    w_value,
    w_alpha,
    w_beta,
    conv_query,
    conv_key,
    conv_value,
    decay_log,
    decay_bias,
    w_outgate,
    out_gain,
    w_out,
    ffn_gain,
    w_gate,
    w_up,
    w_down,
):
    heads = w_alpha.shape[1]
    key_dim, value_dim = heads * KH, heads * VH
    small = jnp.zeros((w_alpha.shape[0], TAIL - 2 * heads), w_alpha.dtype)
    weights = jnp.concatenate([w_query, w_key, w_value, w_alpha, w_beta, small], axis=1)
    filters = jnp.concatenate([conv_query, conv_key, conv_value], axis=1)
    decay_pair = jnp.pad(jnp.stack([decay_log, decay_bias]), ((0, 6), (0, TAIL - heads)))
    gain_row = out_gain[None]

    tokens_other, weights, filters, decay_pair = lax.optimization_barrier(
        (swap(tokens, "col"), weights, filters, decay_pair)
    )
    tokens_half = joined(tokens, tokens_other, "col")
    whole = joined(tokens_half, swap(tokens_half, "row"), "row").astype(jnp.float32)
    normed = rms_scale(whole, norm_gain).astype(jnp.bfloat16)
    proj = plain_product(normed, weights)
    gate = plain_product(normed, w_outgate)
    later, gate = lax.optimization_barrier((cotangent, gate))
    grad_out_half = joined(later, swap(later, "col"), "col")
    mixed, act, inverse, state, delta, result, score, gram, query, step = mixer_forward(
        lengths, proj, gate, filters, decay_pair, gain_row, heads
    )
    mixed, grad_out_half = lax.optimization_barrier((mixed, grad_out_half))
    hidden_half = tokens_half.astype(jnp.float32) + pair_total(
        scatter_step(plain_product(mixed, w_out), "row"), "col"
    )
    hidden_own = half_of(hidden_half, lax.axis_index("col"))
    hidden_low = hidden_half.astype(jnp.bfloat16)
    hidden = joined(hidden_low, swap(hidden_low, "row"), "row").astype(jnp.float32)
    normed_ffn = rms_scale(hidden, ffn_gain).astype(jnp.bfloat16)
    gate_act = plain_product(normed_ffn, w_gate)
    up_act = plain_product(normed_ffn, w_up)
    sigma = jax.nn.sigmoid(gate_act)
    product = (gate_act * sigma * up_act).astype(jnp.bfloat16)
    grad_out = joined(grad_out_half, swap(grad_out_half, "row"), "row")
    grad_product = right_product(grad_out, w_down)
    grad_gate_act = (grad_product * up_act * sigma * (1.0 + gate_act * (1.0 - sigma))).astype(
        jnp.bfloat16
    )
    grad_up_act = (grad_product * gate_act * sigma).astype(jnp.bfloat16)
    grad_normed_ffn = right_product(grad_gate_act, w_gate) + right_product(grad_up_act, w_up)
    grad_hidden_part, grad_ffn_gain = norm_back(hidden, ffn_gain, grad_normed_ffn)
    grad_down = left_product(product, grad_out)
    grad_gate = left_product(normed_ffn, grad_gate_act)
    grad_up = left_product(normed_ffn, grad_up_act)
    ffn_grads = tuple(item.astype(jnp.bfloat16) for item in (grad_down, grad_gate, grad_up))
    grad_hidden_half = (
        grad_out_half.astype(jnp.float32)
        + pair_total(scatter_step(grad_hidden_part, "row"), "col")
    ).astype(jnp.bfloat16)
    grad_hidden_half, *ffn_grads = lax.optimization_barrier((grad_hidden_half, *ffn_grads))
    ffn_sums = lax.psum(tuple(ffn_grads), "dp")
    grad_hidden = joined(grad_hidden_half, swap(grad_hidden_half, "row"), "row")
    grad_hidden_own = half_of(grad_hidden_half, lax.axis_index("col"))
    grad_hidden, product_later = lax.optimization_barrier((grad_hidden, product))
    output = (hidden_own + scatter_features(plain_product(product_later, w_down))).astype(jnp.bfloat16)
    grad_mixed = right_product(grad_hidden, w_out)
    by_y, by_z = (0, 1, 2), (1, 2, 0)
    staged = lax.axis_size("dp") == 8

    def advance(part, step):
        if not staged:
            return part
        if isinstance(part, tuple):
            return tuple(
                totals_step(item, "dp", order, step) for item, order in zip(part, (by_z, by_y))
            )
        return totals_step(part, "dp", by_y, step)

    grad_gate_proj, gain_grad, back, reach = gate_backward(
        grad_mixed, gate, gain_row, result, query, step, heads
    )
    out_part = left_product(grad_hidden, mixed)
    gate_part = left_product(normed, grad_gate_proj)
    out_part, gate_part, back = lax.optimization_barrier((out_part, gate_part, back))
    early = jnp.concatenate([advance(out_part, 0), advance(gate_part, 0)], axis=1)
    grad_proj, filter_grad, decay_grad = rule_backward(
        lengths, proj, filters, decay_pair, (act, inverse, state, delta, score, gram), back, reach, heads
    )
    conv_dim = 2 * key_dim + value_dim
    early, grad_proj = lax.optimization_barrier((early, grad_proj))
    late = left_product(normed, grad_proj[:, :conv_dim])
    early, late = lax.optimization_barrier((early, late))
    late = (late[:, : 2 * key_dim], late[:, 2 * key_dim :])
    early, late = advance(early, 1), advance(late, 0)
    early, late, grad_proj = lax.optimization_barrier((early, late, grad_proj))

    early, late = advance(early, 2), advance(late, 1)
    grad_pair = left_product(normed, grad_proj[:, conv_dim:])
    grad_normed = right_product(grad_proj, weights) + right_product(grad_gate_proj, w_outgate)
    grad_input_part, grad_norm_gain = norm_back(whole, norm_gain, grad_normed)
    grad_input_part = grad_input_part.astype(jnp.bfloat16)
    early, late, grad_input_part, grad_norm_gain, grad_pair = lax.optimization_barrier(
        (early, late, grad_input_part, grad_norm_gain, grad_pair)
    )

    early, late = advance(early, 3), advance(late, 2)
    gains = jnp.concatenate([grad_norm_gain, grad_ffn_gain, gain_grad[0]])
    corner = lax.ppermute(gains, ("row", "col"), [(0, 3), (1, 2), (2, 1), (3, 0)])
    gains = (gains + swap(gains, "row")) + (swap(gains, "col") + corner)
    sizes = (
        gains,
        filter_grad.reshape(-1),
        grad_pair[:, : 2 * heads].reshape(-1),
        decay_grad[:2, :heads].reshape(-1),
    )
    small_sum = jnp.concatenate(sizes)
    input_row = scatter_step(grad_input_part.astype(jnp.float32), "row")
    early, late, small_sum, input_row = lax.optimization_barrier(
        (early, late, small_sum, input_row)
    )

    early, late = advance(early, 4), advance(late, 3)
    small_sum = small_step(small_sum, "dp", 0)
    input_grad = (
        grad_hidden_own.astype(jnp.float32) + scatter_step(input_row, "col")
    ).astype(jnp.bfloat16)
    early, late, small_sum, input_grad, *ffn_sums = lax.optimization_barrier(
        (early, late, small_sum, input_grad, *ffn_sums)
    )

    late = advance(late, 4)
    if staged:
        corner = lax.ppermute(small_sum, "dp", [(place, place ^ 6) for place in range(8)])
        small_sum = (small_sum + bit_swap(small_sum, "dp", 1)) + (
            bit_swap(small_sum, "dp", 2) + corner
        )
    if not staged:
        small_sum = lax.psum(small_sum, "dp")
        early, *late = (
            item.astype(jnp.float32)
            for item in lax.psum(
                tuple(item.astype(jnp.bfloat16) for item in (early, *late)), "dp"
            )
        )
    out_sum = early[:, :value_dim].T
    gate_weight_sum = early[:, value_dim:]
    pair_sum, value_sum = late
    query_sum, key_sum = pair_sum[:, :key_dim], pair_sum[:, key_dim:]
    down_sum, gate_sum, up_sum = (item.astype(jnp.float32) for item in ffn_sums)
    width = norm_gain.shape[0]
    places = [0]
    for item in sizes:
        places.append(places[-1] + item.shape[0])
    pieces = [small_sum[low:high] for low, high in zip(places, places[1:])]
    filter_sum = pieces[1].reshape(filters.shape)
    rate_sum = pieces[2].reshape(-1, 2 * heads)
    decay_sum = pieces[3].reshape(2, heads)
    return (
        output,
        input_grad,
        pieces[0][:width],
        query_sum,
        key_sum,
        value_sum,
        rate_sum[:, :heads],
        rate_sum[:, heads:],
        filter_sum[:, :key_dim],
        filter_sum[:, key_dim : 2 * key_dim],
        filter_sum[:, 2 * key_dim :],
        decay_sum[0],
        decay_sum[1],
        gate_weight_sum,
        pieces[0][2 * width :],
        out_sum,
        pieces[0][width : 2 * width],
        gate_sum,
        up_sum,
        down_sum,
    )


def solution(mesh):
    placed = (
        P("dp", ("row", "col")),
        P("dp", ("row", "col")),
        P("dp", None),
        P(),
        P(None, ("row", "col")),
        P(None, ("row", "col")),
        P(None, ("row", "col")),
        P(None, ("row", "col")),
        P(None, ("row", "col")),
        P(None, ("row", "col")),
        P(None, ("row", "col")),
        P(None, ("row", "col")),
        P(("row", "col")),
        P(("row", "col")),
        P(None, ("row", "col")),
        P(),
        P(("row", "col"), None),
        P(),
        P(None, ("row", "col")),
        P(None, ("row", "col")),
        P(("row", "col"), None),
    )
    return jax.shard_map(
        body,
        mesh=mesh,
        in_specs=placed,
        out_specs=(
            P("dp", ("row", "col")),
            P("dp", ("row", "col")),
            P(),
            P(None, ("row", "col")),
            P(None, ("row", "col")),
            P(None, ("row", "col")),
            P(None, ("row", "col")),
            P(None, ("row", "col")),
            P(None, ("row", "col")),
            P(None, ("row", "col")),
            P(None, ("row", "col")),
            P(("row", "col")),
            P(("row", "col")),
            P(None, ("row", "col")),
            P(),
            P(("row", "col"), None),
            P(),
            P(None, ("row", "col")),
            P(None, ("row", "col")),
            P(("row", "col"), None),
        ),
        check_vma=False,
    )
```
